32 devices in a mesh: groups: 2 (over y), row: 4 (over z), col: 2 (over core), chan: 2 (over x).
Axes of the slice: x: 2, y: 2, z: 4, core: 2. Of those that a mesh axis runs over, the one named last changes fastest.
Arguments:
- pair: bfloat16 [48, 24, 128], P(('groups', 'row'), 'col', 'chan'), parts along dimension 0, may hold values from -6 to 6
- token_mask: int32 [48], P('groups'), parts along dimension 0, may hold values 0 or 1
- w_in: bfloat16 [128, 4, 128], P(None, None, 'chan'), may hold values from -0.5 to 0.5
- w_gate: bfloat16 [128, 128], P(None, 'chan'), may hold values from -0.5 to 0.5
- w_out: bfloat16 [128, 128], P('chan'), may hold values from -0.5 to 0.5
- cotangent: bfloat16 [48, 24, 128], P(('groups', 'row'), 'col', 'chan'), parts along dimension 0, may hold values from -6 to 6
Outputs:
- update: bfloat16 [48, 24, 128], P(('groups', 'row'), 'col', 'chan'), parts along dimension 0
- pair_grad: bfloat16 [48, 24, 128], P(('groups', 'row'), 'col', 'chan'), parts along dimension 0
The draws below stay inside these ranges and needn't reach their ends.
There are 2 independent parts, one for each index of `groups`. The reference program is written for one: setup_inputs(seed, part) draws one part's arguments, and reference() takes and returns one part's arrays. A program takes and returns all parts, laid end to end along the dimension named above; an argument that names none is the same for every part. Nothing has to cross between parts.
Inputs may be any that keep to these rules, and one draw needn't show every extreme that they name: `token_mask`: 1 marks a real token, 0 padding.
All inputs are finite; a program needn't handle non-finite values.
Results may differ from the reference program's by a relative error of at most 0.008.
Values may be sent and summed in bfloat16 or wider, within the bound.
A program may use at most 64 MiB of HBM per device.

```python
import jax
import jax.numpy as jnp
from jax import lax

C = 128
HIDDEN_WIDTH = 128
N = 24


def set_ends(entries, stream_key, least, largest):
    shape = entries.shape
    place = [jax.random.randint(jax.random.fold_in(stream_key, axis), (), 0, shape[axis]) for axis in range(len(shape))]
    entries = entries.at[tuple(place)].set(least)
    longest = shape.index(max(shape))
    place[longest] = (place[longest] + 1) % shape[longest]
    return entries.at[tuple(place)].set(largest)


def levels(own_key, dims, cuts, low, high):
    def one(axis_at, parts):
        draws = jax.random.uniform(jax.random.fold_in(jax.random.fold_in(own_key, 6), axis_at), (parts,), jnp.float32, low / len(cuts), high / len(cuts))
        return jnp.repeat(jnp.exp(draws), dims[axis_at] // parts).reshape((-1,) + (1,) * (len(dims) - axis_at - 1))

    gain = one(*cuts[0])
    for cut in cuts[1:]:
        gain = gain * one(*cut)
    return gain


def scatter_about(stream_key, dims, scale, most, pieces=(), held_as=jnp.bfloat16):
    loudness = levels(stream_key, dims, pieces, -0.22, 0.18) if pieces else 1.0
    values = jax.random.normal(stream_key, dims, jnp.float32) * scale * loudness
    return jnp.minimum(jnp.maximum(values, -most), most).astype(held_as)


def setup_inputs(seed: int = 0, part: int = 0) -> dict:
    seeds = jax.random.split(jax.random.key(seed), 7)
    part_splits = jax.random.split(jax.random.fold_in(seeds[6], part), 7)
    return {
        "pair": scatter_about(part_splits[0], (N, N, C), 1.0, 6.0, ((0, 4), (1, 2), (2, 2))),
        "token_mask": set_ends((jax.random.randint(part_splits[1], (N,), 0, 8) < 7).astype(jnp.int32), jax.random.fold_in(part_splits[1], 1), 0, 1),
        "w_in": scatter_about(seeds[2], (C, 4, HIDDEN_WIDTH), C ** -0.5, 0.5, ((2, 2),)),
        "w_gate": scatter_about(seeds[3], (C, C), C ** -0.5, 0.5, ((1, 2),)),
        "w_out": scatter_about(seeds[4], (HIDDEN_WIDTH, C), HIDDEN_WIDTH ** -0.5, 0.5, ((0, 2),)),
        "cotangent": scatter_about(part_splits[5], (N, N, C), 1.0, 6.0, ((0, 4), (1, 2), (2, 2))),
    }


EPS = 1e-05

def norm_stats(values, width):
    mean = lax.optimization_barrier(jnp.sum(values, axis=-1, keepdims=True)) / width
    square = lax.optimization_barrier(jnp.sum(values * values, axis=-1, keepdims=True)) / width
    return (mean, lax.rsqrt(square - mean * mean + EPS))

def reference(pair, token_mask, w_in, w_gate, w_out, cotangent):
    f32 = jnp.float32
    brain_float_half = jnp.bfloat16
    zfull = pair.astype(f32)
    mean_z, rstd_z = norm_stats(zfull, C)
    zhat = (zfull - mean_z) * rstd_z
    zn_b = zhat.astype(brain_float_half)
    proj = jnp.einsum('ijc,cqh->ijqh', zn_b.astype(f32), w_in.astype(f32))
    maskf = token_mask.astype(f32)
    pmask = (maskf[:, None] * maskf[None, :])[..., None]
    sig_one = jax.nn.sigmoid(proj[:, :, 1])
    sig_three = jax.nn.sigmoid(proj[:, :, 3])
    left = (pmask * sig_one * proj[:, :, 0]).astype(brain_float_half)
    right = (pmask * sig_three * proj[:, :, 2]).astype(brain_float_half)
    triangle_product = jnp.einsum('ikh,jkh->ijh', left.astype(f32), right.astype(f32))
    input_mean, input_inverse_deviation = norm_stats(triangle_product, HIDDEN_WIDTH)
    centered_input = (triangle_product - input_mean) * input_inverse_deviation
    normed_input_low_precision = centered_input.astype(brain_float_half)
    proj_out = jnp.einsum('ijh,hc->ijc', normed_input_low_precision.astype(f32), w_out.astype(f32))
    gate = jax.nn.sigmoid(jnp.einsum('ijd,dc->ijc', zn_b.astype(f32), w_gate.astype(f32)))
    update = (gate * proj_out).astype(brain_float_half)
    cot = cotangent.astype(f32)
    dproj = (cot * gate).astype(brain_float_half)
    dgate = (cot * proj_out * gate * (1.0 - gate)).astype(brain_float_half)
    normed_input_gradient = jnp.einsum('ijc,hc->ijh', dproj.astype(f32), w_out.astype(f32))
    first_operand = lax.optimization_barrier(jnp.sum(normed_input_gradient, axis=-1, keepdims=True)) / HIDDEN_WIDTH
    second_operand = lax.optimization_barrier(jnp.sum(normed_input_gradient * centered_input, axis=-1, keepdims=True)) / HIDDEN_WIDTH
    triangle_gradient = ((normed_input_gradient - first_operand - centered_input * second_operand) * input_inverse_deviation).astype(brain_float_half)
    dleft = jnp.einsum('ijh,jkh->ikh', triangle_gradient.astype(f32), right.astype(f32))
    dright = jnp.einsum('ijh,ikh->jkh', triangle_gradient.astype(f32), left.astype(f32))
    dpre = jnp.stack([dleft * pmask * sig_one, dleft * pmask * proj[:, :, 0] * sig_one * (1.0 - sig_one), dright * pmask * sig_three, dright * pmask * proj[:, :, 2] * sig_three * (1.0 - sig_three)], axis=2).astype(brain_float_half)
    dzn = jnp.einsum('ijqh,cqh->ijc', dpre.astype(f32), w_in.astype(f32))
    dzn = dzn + jnp.einsum('ijd,cd->ijc', dgate.astype(f32), w_gate.astype(f32))
    first_z = lax.optimization_barrier(jnp.sum(dzn, axis=-1, keepdims=True)) / C
    second_z = lax.optimization_barrier(jnp.sum(dzn * zhat, axis=-1, keepdims=True)) / C
    pair_grad = ((dzn - first_z - zhat * second_z) * rstd_z).astype(brain_float_half)
    return (update, pair_grad)
```

```python
import functools

import jax
import jax.numpy as jnp
from jax import lax
from jax.experimental import pallas as pl
from jax.experimental.pallas import tpu as pltpu
from jax.sharding import PartitionSpec as P

EPS = 1e-05
MESH = pl.DeviceIdType.MESH


def sigmoid(x):
    return 1.0 / (1.0 + jnp.exp(-x))


def lane_mean(x):
    return jnp.sum(x, axis=-1, keepdims=True) * (1.0 / x.shape[-1])


def norm_stats(x):
    mean = lane_mean(x)
    return mean, lax.rsqrt(lane_mean(x * x) - mean * mean + EPS)


def merge(first, second):
    first, second = first.astype(jnp.float32), second.astype(jnp.float32)
    axis = first.ndim - 1
    width = first.shape[-1]
    low = lax.broadcasted_iota(jnp.int32, first.shape, axis) < width // 2
    return (
        jnp.where(low, first, pltpu.roll(second, width // 2, axis)),
        jnp.where(low, pltpu.roll(first, width // 2, axis), second),
    )


def dot(a, b, transposed=False):
    return lax.dot_general(
        a, b, (((1,), (1 if transposed else 0,)), ((), ())), preferred_element_type=jnp.float32
    )


def kernel(
    n_row, pair_ref, mask_ref, w_in_ref, w_gate_ref, w_out_ref, cot_ref, update_ref, grad_ref,
    pbuf, cbuf, wbuf, z_s, zh_s, c_s, l_s, r_s, mj_s, u_s, dg_s, da_s, db_s,
    p_send, p_fwd, p_recv, c_send, c_fwd, c_recv, w_send, w_recv,
):
    f32, bf16 = jnp.float32, jnp.bfloat16
    rows, cols, _ = pair_ref.shape
    n = rows * n_row
    width = 2 * pair_ref.shape[2]
    half_rows = rows // 2
    pad = pbuf.shape[4]
    block = rows * n
    r, c, h = lax.axis_index("row"), lax.axis_index("col"), lax.axis_index("chan")
    other_c, other_h = 1 - c, 1 - h

    def place(dr, dh):
        return lax.rem(r + dr, n_row), lax.rem(h + dh, 2)

    steps = [(dr, dh) for dr in range(n_row) for dh in range(2)]
    far = [s for s in steps if s != (0, 0)]

    barrier = pltpu.get_barrier_semaphore()
    for dr, dh in far:
        pr, ph = place(dr, dh)
        pl.semaphore_signal(barrier, inc=1, device_id={"row": pr, "chan": ph}, device_id_type=MESH)
    pl.semaphore_signal(barrier, inc=1, device_id={"col": other_c}, device_id_type=MESH)

    def pack(ref, buf):
        x = ref[...].astype(f32)
        x = jnp.concatenate([x[:half_rows], x[half_rows:]], axis=-1)
        buf[r, c, h] = jnp.zeros(buf.shape[3:], bf16)
        buf[r, c, h, :, 0:cols, :] = x.astype(bf16)

    pack(pair_ref, pbuf)
    for p in range(2):
        wbuf[h, p, 0:width, :] = jnp.concatenate([w_in_ref[2 * p], w_in_ref[2 * p + 1]], axis=-1)
    wg = w_gate_ref[...]
    wbuf[h, 0, width : width + width // 2, :] = jnp.concatenate(
        [wg[: width // 2], wg[width // 2 :]], axis=-1
    )
    wbuf[h, 1, width : width + width // 2, :] = w_out_ref[...]
    pack(cot_ref, cbuf)
    pl.semaphore_wait(barrier, len(far) + 1)

    def far_copy(buf, slot, send, recv, device):
        return pltpu.make_async_remote_copy(
            src_ref=buf.at[slot], dst_ref=buf.at[slot], send_sem=send, recv_sem=recv,
            device_id=device, device_id_type=MESH,
        )

    def spread(buf, send, fwd, recv):
        sent = []
        own = (r, c, h)
        for dr, dh in far:
            pr, ph = place(dr, dh)
            sent.append(
                far_copy(buf, own, send.at[dr, dh], recv.at[own], {"row": pr, "chan": ph})
            )
        sent.append(far_copy(buf, own, fwd.at[0, 0], recv.at[own], {"col": other_c}))
        for copy in sent:
            copy.start()
        return sent

    def relay(buf, fwd, recv):
        sent = []
        for dr, dh in far:
            pr, ph = place(dr, dh)
            slot = (pr, c, ph)
            copy = far_copy(buf, slot, fwd.at[dr, dh], recv.at[slot], {"col": other_c})
            copy.wait_recv()
            copy.start()
            sent.append(copy)
        return sent

    def arrived(buf, fwd, recv):
        for dr, dh in steps:
            pr, ph = place(dr, dh)
            slot = (pr, other_c, ph)
            far_copy(buf, slot, fwd.at[dr, dh], recv.at[slot], {"col": other_c}).wait_recv()

    sent = spread(pbuf, p_send, p_fwd, p_recv)
    w_far = far_copy(wbuf, (h, c), w_send.at[0], w_recv.at[0], {"chan": other_h})
    w_far.start()
    sent += spread(cbuf, c_send, c_fwd, c_recv)

    token = lax.broadcasted_iota(jnp.int32, (n, width), 0)
    mj = jnp.zeros((n, width), f32)
    for j in range(n):
        mj = jnp.where(token == j, mask_ref[j].astype(f32), mj)
    mj_s[...] = jnp.zeros(mj_s.shape, f32)
    mj_s[0:n, :] = mj
    tail = z_s.shape[0] - n * n
    for s in (z_s, zh_s, l_s, r_s):
        s[n * n : n * n + tail, :] = jnp.zeros((tail, width), f32)

    sent += relay(pbuf, p_fwd, p_recv)
    w_near = far_copy(wbuf, (other_h, c), w_send.at[1], w_recv.at[1], {"col": other_c})
    far_copy(wbuf, (other_h, c), w_send.at[0], w_recv.at[0], {"chan": other_h}).wait_recv()
    w_near.start()
    sent += [w_far, w_near]
    arrived(pbuf, p_fwd, p_recv)
    far_copy(wbuf, (other_h, other_c), w_send.at[1], w_recv.at[1], {"col": other_c}).wait_recv()

    w_in = []
    for p in range(2):
        w_in += [w.astype(bf16) for w in merge(wbuf[0, p, 0:width, :], wbuf[1, p, 0:width, :])]
    last = slice(width, width + width // 2)
    w_gate = jnp.concatenate(merge(wbuf[0, 0, last, :], wbuf[1, 0, last, :]), axis=0).astype(bf16)
    w_out = jnp.concatenate([wbuf[0, 1, last, :], wbuf[1, 1, last, :]], axis=0)

    def unpack(buf, dst, br):
        for bc in range(2):
            for part, full in enumerate(merge(buf[br, bc, 0], buf[br, bc, 1])):
                for t in range(half_rows):
                    start = (br * rows + part * half_rows + t) * n + bc * cols
                    dst[start : start + cols, :] = full[t, 0:cols, :]

    for br in range(n_row):
        unpack(pbuf, z_s, br)
        at = slice(br * block, (br + 1) * block)
        z = z_s[at, :]
        mean, rstd = norm_stats(z)
        zh = (z - mean) * rstd
        zh_s[at, :] = zh
        zn = zh.astype(bf16)
        pm = jnp.concatenate([mj * mask_ref[br * rows + t].astype(f32) for t in range(rows)], axis=0)
        left = pm * sigmoid(dot(zn, w_in[1])) * dot(zn, w_in[0])
        l_s[at, :] = left.astype(bf16).astype(f32)
        right = pm * sigmoid(dot(zn, w_in[3])) * dot(zn, w_in[2])
        r_s[at, :] = right.astype(bf16).astype(f32)

    sent += relay(cbuf, c_fwd, c_recv)

    def products(rows_ref, turned_ref):
        def step(k, sums):
            turned = turned_ref[pl.ds(k, n, stride=n), :]
            return tuple(
                s + rows_ref[pl.ds((r * rows + i) * n + k, 1), :] * turned
                for i, s in enumerate(sums)
            )

        sums = lax.fori_loop(0, n, step, (jnp.zeros((n, width), f32),) * rows, unroll=4)
        return jnp.concatenate(sums, axis=0)

    tri_a = products(l_s, r_s)
    tri_b = products(r_s, l_s)

    arrived(cbuf, c_fwd, c_recv)
    for br in range(n_row):
        unpack(cbuf, c_s, br)

    def turned_block(ref):
        return jnp.concatenate(
            [ref[pl.ds(r * rows + j, n, stride=n), :] for j in range(rows)], axis=0
        )

    def hidden(tri, zn, cot):
        mean, rstd = norm_stats(tri)
        xhat = (tri - mean) * rstd
        proj_out = dot(xhat.astype(bf16), w_out)
        gate = sigmoid(dot(zn, w_gate))
        dxn = dot((cot * gate).astype(bf16), w_out, True)
        dtri = (dxn - lane_mean(dxn) - xhat * lane_mean(dxn * xhat)) * rstd
        return proj_out, gate, dtri.astype(bf16).astype(f32)

    own_rows = pl.ds(pl.multiple_of(r * block, 8), block)
    cot_a = c_s[own_rows, :]
    proj_out, gate, dtri = hidden(tri_a, zh_s[own_rows, :].astype(bf16), cot_a)
    da_s[...] = dtri
    u_s[...] = jnp.zeros(u_s.shape, f32)
    dg_s[...] = jnp.zeros(dg_s.shape, f32)
    u_s[0:block, :] = gate * proj_out
    dg_s[0:block, :] = cot_a * proj_out * gate * (1.0 - gate)
    _, _, dtri = hidden(tri_b, turned_block(zh_s).astype(bf16), turned_block(c_s))
    db_s[...] = dtri

    def own_cells(ref, first):
        return jnp.concatenate(
            [ref[pl.ds((first + i) * n + c * cols, pad), :] for i in range(rows)], axis=0
        )

    def gradients(d_ref, other_ref):
        def step(j, sums):
            other = other_ref[pl.ds(j * n + c * cols, pad), :]
            return tuple(s + d_ref[pl.ds(i * n + j, 1), :] * other for i, s in enumerate(sums))

        sums = lax.fori_loop(0, n, step, (jnp.zeros((pad, width), f32),) * rows, unroll=4)
        return jnp.concatenate(sums, axis=0)

    dleft = gradients(da_s, r_s)
    dright = gradients(db_s, l_s)

    z = own_cells(z_s, r * rows)
    mean, rstd = norm_stats(z)
    zhat = (z - mean) * rstd
    zn = zhat.astype(bf16)
    own_mask = mj_s[pl.ds(c * cols, pad), :]
    pm = jnp.concatenate(
        [own_mask * mask_ref[r * rows + i].astype(f32) for i in range(rows)], axis=0
    )
    s1, s3 = sigmoid(dot(zn, w_in[1])), sigmoid(dot(zn, w_in[3]))
    dpre = [
        dleft * pm * s1,
        dleft * pm * dot(zn, w_in[0]) * s1 * (1.0 - s1),
        dright * pm * s3,
        dright * pm * dot(zn, w_in[2]) * s3 * (1.0 - s3),
    ]
    dzn = dot(own_cells(dg_s, 0).astype(bf16), w_gate, True)
    for q in range(4):
        dzn = dzn + dot(dpre[q].astype(bf16), w_in[q], True)
    grad = (dzn - lane_mean(dzn) - zhat * lane_mean(dzn * zhat)) * rstd

    def put(ref, value):
        value = jnp.where(h == 0, value, pltpu.roll(value, width // 2, 1))
        value = value.reshape(rows, pad, width)[:, 0:cols, 0 : width // 2]
        ref[...] = value.astype(bf16)

    put(update_ref, own_cells(u_s, 0))
    put(grad_ref, grad)
    for copy in sent:
        copy.wait_send()


def gathered(n_row, pair, token_mask, w_in, w_gate, w_out, cotangent):
    f32, bf16 = jnp.float32, jnp.bfloat16
    rows, cols, chans = pair.shape
    n = rows * n_row
    width = 2 * chans
    pad = -(-cols // 16) * 16
    vmem = pl.BlockSpec(memory_space=pltpu.VMEM)
    shards = pltpu.VMEM((n_row, 2, 2, rows // 2, pad, width), bf16)
    cells = pltpu.VMEM((n * n + 8, width), f32)
    block = pltpu.VMEM((rows * n, width), f32)
    block_and_tail = pltpu.VMEM((rows * n + 8, width), f32)
    dma = pltpu.SemaphoreType.DMA
    out = jax.ShapeDtypeStruct(pair.shape, bf16)
    return pl.pallas_call(
        functools.partial(kernel, n_row),
        out_shape=(out, out),
        in_specs=[vmem, pl.BlockSpec(memory_space=pltpu.SMEM), vmem, vmem, vmem, vmem],
        out_specs=(vmem, vmem),
        scratch_shapes=[
            shards, shards, pltpu.VMEM((2, 2, width + width // 2, width), bf16),
            cells, cells, cells, cells, cells, pltpu.VMEM((n + 8, width), f32),
            block_and_tail, block_and_tail, block, block,
            dma((n_row, 2)), dma((n_row, 2)), dma((n_row, 2, 2)),
            dma((n_row, 2)), dma((n_row, 2)), dma((n_row, 2, 2)),
            dma((2,)), dma((2,)),
        ],
        compiler_params=pltpu.CompilerParams(
            collective_id=0, has_side_effects=True, vmem_limit_bytes=24 * 2**20
        ),
    )(pair, token_mask, w_in.transpose(1, 0, 2), w_gate, w_out, cotangent)


def body(pair, token_mask, w_in, w_gate, w_out, cotangent):
    f32 = jnp.float32
    brain_float_half = jnp.bfloat16
    rows = pair.shape[0]
    cols = pair.shape[1]
    chans = pair.shape[2]
    width_c = w_in.shape[0]
    hidden_dev = w_in.shape[2]
    hidden_channel_width = hidden_dev * lax.axis_size("chan")
    row_start = lax.axis_index("row") * rows
    col_start = lax.axis_index("col") * cols
    chan_start = lax.axis_index("chan") * chans
    zfull = lax.all_gather(pair, "chan", axis=2, tiled=True).astype(f32)
    mean_z = jnp.sum(zfull, axis=-1, keepdims=True) / width_c
    square_z = jnp.sum(zfull * zfull, axis=-1, keepdims=True) / width_c
    rstd_z = lax.rsqrt(square_z - mean_z * mean_z + EPS)
    zhat = (zfull - mean_z) * rstd_z
    zn_b = zhat.astype(brain_float_half)
    proj = jnp.einsum("rkc,cqh->rkqh", zn_b, w_in, preferred_element_type=f32)
    maskf = token_mask.astype(f32)
    mask_rows = lax.dynamic_slice_in_dim(maskf, row_start, rows)
    mask_cols = lax.dynamic_slice_in_dim(maskf, col_start, cols)
    pmask = (mask_rows[:, None] * mask_cols[None, :])[..., None]
    sig_one = jax.nn.sigmoid(proj[:, :, 1])
    sig_three = jax.nn.sigmoid(proj[:, :, 3])
    left = (pmask * sig_one * proj[:, :, 0]).astype(brain_float_half)
    right = (pmask * sig_three * proj[:, :, 2]).astype(brain_float_half)
    partial_tri = jnp.einsum(
        "ikh,jkh->ijh",
        left,
        lax.all_gather(right, "row", axis=0, tiled=True),
        preferred_element_type=f32,
    )
    triangle_product = lax.psum_scatter(partial_tri, "col", scatter_dimension=1, tiled=True)
    sum_x, square_x = lax.psum(
        (jnp.sum(triangle_product, axis=-1), jnp.sum(triangle_product * triangle_product, axis=-1)),
        "chan",
    )
    input_mean = (sum_x / hidden_channel_width)[..., None]
    input_inverse_deviation = lax.rsqrt(
        square_x[..., None] / hidden_channel_width - input_mean * input_mean + EPS
    )
    centered_input = (triangle_product - input_mean) * input_inverse_deviation
    normed_input_low_precision = centered_input.astype(brain_float_half)
    out_term = jnp.einsum(
        "rch,hd->rcd", normed_input_low_precision, w_out, preferred_element_type=f32
    )
    proj_out = lax.psum_scatter(out_term, "chan", scatter_dimension=2, tiled=True)
    gate = jax.nn.sigmoid(jnp.einsum("rcd,de->rce", zn_b, w_gate, preferred_element_type=f32))
    update = (gate * proj_out).astype(brain_float_half)
    cot = cotangent.astype(f32)
    dproj = (cot * gate).astype(brain_float_half)
    dgate = (cot * proj_out * gate * (1.0 - gate)).astype(brain_float_half)
    dproj_all = lax.all_gather(dproj, "chan", axis=2, tiled=True)
    normed_input_gradient = jnp.einsum("rcd,hd->rch", dproj_all, w_out, preferred_element_type=f32)
    first_operand, second_operand = lax.psum(
        (
            jnp.sum(normed_input_gradient, axis=-1),
            jnp.sum(normed_input_gradient * centered_input, axis=-1),
        ),
        "chan",
    )
    triangle_gradient = (
        (
            normed_input_gradient
            - (first_operand / hidden_channel_width)[..., None]
            - centered_input * (second_operand / hidden_channel_width)[..., None]
        )
        * input_inverse_deviation
    ).astype(brain_float_half)
    dtri_rows = lax.all_gather(triangle_gradient, "col", axis=1, tiled=True)
    block = dtri_rows
    dleft = jnp.einsum(
        "ijh,jkh->ikh",
        block,
        lax.all_gather(right, "row", axis=0, tiled=True),
        preferred_element_type=f32,
    )
    dtri_turned = lax.all_to_all(dtri_rows, "row", split_axis=1, concat_axis=0, tiled=True)
    block = dtri_turned
    dright = jnp.einsum(
        "ijh,ikh->jkh",
        block,
        lax.all_gather(left, "row", axis=0, tiled=True),
        preferred_element_type=f32,
    )
    dpre = jnp.stack(
        [
            dleft * pmask * sig_one,
            dleft * pmask * proj[:, :, 0] * sig_one * (1.0 - sig_one),
            dright * pmask * sig_three,
            dright * pmask * proj[:, :, 2] * sig_three * (1.0 - sig_three),
        ],
        axis=2,
    ).astype(brain_float_half)
    dzn_term = jnp.einsum("rkqh,cqh->rkc", dpre, w_in, preferred_element_type=f32)
    dzn_term = dzn_term + jnp.einsum("rkd,cd->rkc", dgate, w_gate, preferred_element_type=f32)
    dzn = lax.psum_scatter(dzn_term, "chan", scatter_dimension=2, tiled=True)
    zhat_own = lax.dynamic_slice_in_dim(zhat, chan_start, chans, 2)
    first_z, second_z = lax.psum((jnp.sum(dzn, axis=-1), jnp.sum(dzn * zhat_own, axis=-1)), "chan")
    pair_grad = (
        (dzn - (first_z / width_c)[..., None] - zhat_own * (second_z / width_c)[..., None]) * rstd_z
    ).astype(brain_float_half)
    return (update, pair_grad)


def plan(pair, token_mask, w_in, w_gate, w_out, cotangent):
    n_row, n_col, n_chan = (lax.axis_size(a) for a in ("row", "col", "chan"))
    rows, cols, chans = pair.shape
    n = token_mask.shape[0]
    small = n <= 32 and n % 8 == 0 and rows % 2 == 0 and cols % 4 == 0 and rows * n % 16 == 0
    shaped = n_col == 2 and n_chan == 2 and chans == 64 and w_in.shape == (128, 4, 64)
    if small and shaped and -(-cols // 16) * 16 - cols <= 8:
        return gathered(n_row, pair, token_mask, w_in, w_gate, w_out, cotangent)
    return body(pair, token_mask, w_in, w_gate, w_out, cotangent)


def solution(mesh):
    return jax.shard_map(
        plan,
        mesh=mesh,
        in_specs=(
            P(("groups", "row"), "col", "chan"),
            P("groups"),
            P(None, None, "chan"),
            P(None, "chan"),
            P("chan", None),
            P(("groups", "row"), "col", "chan"),
        ),
        out_specs=(P(("groups", "row"), "col", "chan"), P(("groups", "row"), "col", "chan")),
        check_vma=False,
    )
```

```python
import functools

import jax
import jax.numpy as jnp
from jax import lax
from jax.experimental import pallas as pl
from jax.experimental.pallas import tpu as pltpu
from jax.sharding import PartitionSpec as P

EPS = 1e-05
MESH = pl.DeviceIdType.MESH


def sigmoid(x):
    return 1.0 / (1.0 + jnp.exp(-x))


def lane_mean(x):
    return jnp.sum(x, axis=-1, keepdims=True) * (1.0 / x.shape[-1])


def norm_stats(x):
    mean = lane_mean(x)
    return mean, lax.rsqrt(lane_mean(x * x) - mean * mean + EPS)


def merge(first, second):
    first, second = first.astype(jnp.float32), second.astype(jnp.float32)
    axis = first.ndim - 1
    width = first.shape[-1]
    low = lax.broadcasted_iota(jnp.int32, first.shape, axis) < width // 2
    return (
        jnp.where(low, first, pltpu.roll(second, width // 2, axis)),
        jnp.where(low, pltpu.roll(first, width // 2, axis), second),
    )


def dot(a, b, transposed=False):
    return lax.dot_general(
        a, b, (((1,), (1 if transposed else 0,)), ((), ())), preferred_element_type=jnp.float32
    )


def kernel(
    n_row, pair_hbm, mask_hbm, w_in_hbm, w_gate_hbm, w_out_hbm, cot_hbm, out_ref,
    pair_ref, cot_ref, mask_ref, in_sem, pbuf, cbuf, wbuf, z_s, zh_s, c_s, l_s, r_s, mj_s, u_s, dg_s, da_s, db_s,
    p_send, p_fwd, p_recv, c_send, c_fwd, c_recv, w_send, w_recv,
):
    f32, bf16 = jnp.float32, jnp.bfloat16
    rows, cols, _ = pair_ref.shape
    n = rows * n_row
    width = 2 * pair_ref.shape[2]
    half_rows = rows // 2
    pad = pbuf.shape[4]
    block = rows * n
    r, c, h = lax.axis_index("row"), lax.axis_index("col"), lax.axis_index("chan")
    other_c, other_h = 1 - c, 1 - h

    def place(dr, dh):
        return lax.rem(r + dr, n_row), lax.rem(h + dh, 2)

    steps = [(dr, dh) for dr in range(n_row) for dh in range(2)]
    far = [s for s in steps if s != (0, 0)]

    mine = pl.ds(pl.multiple_of(h * (width // 2), width // 2), width // 2)
    loads = [
        pltpu.make_async_copy(src, dst, in_sem.at[i])
        for i, (src, dst) in enumerate(
            [
                (pair_hbm, pair_ref),
                (w_in_hbm.at[0:2], wbuf.at[0:2, mine]),
                (w_gate_hbm, wbuf.at[2, mine]),
                (w_in_hbm.at[2:4], wbuf.at[3:5, mine]),
                (w_out_hbm, wbuf.at[5, mine]),
                (cot_hbm, cot_ref),
                (mask_hbm, mask_ref),
            ]
        )
    ]
    for load in loads:
        load.start()

    barrier = pltpu.get_barrier_semaphore()
    for dr, dh in far:
        pr, ph = place(dr, dh)
        pl.semaphore_signal(barrier, inc=1, device_id={"row": pr, "chan": ph}, device_id_type=MESH)
    pl.semaphore_signal(barrier, inc=1, device_id={"col": other_c}, device_id_type=MESH)

    def pack(ref, buf):
        x = ref[...].astype(f32)
        x = jnp.concatenate([x[:half_rows], x[half_rows:]], axis=-1)
        buf[r, c, h] = jnp.zeros(buf.shape[3:], bf16)
        buf[r, c, h, :, 0:cols, :] = x.astype(bf16)

    loads[0].wait()
    pack(pair_ref, pbuf)
    pl.semaphore_wait(barrier, len(far) + 1)

    def far_copy(buf, slot, send, recv, device):
        return pltpu.make_async_remote_copy(
            src_ref=buf.at[slot], dst_ref=buf.at[slot], send_sem=send, recv_sem=recv,
            device_id=device, device_id_type=MESH,
        )

    def spread(buf, send, fwd, recv):
        sent = []
        own = (r, c, h)
        for dr, dh in far:
            pr, ph = place(dr, dh)
            sent.append(
                far_copy(buf, own, send.at[dr, dh], recv.at[own], {"row": pr, "chan": ph})
            )
        sent.append(far_copy(buf, own, fwd.at[0, 0], recv.at[own], {"col": other_c}))
        for copy in sent:
            copy.start()
        return sent

    def relay(buf, fwd, recv):
        sent = []
        for dr, dh in far:
            pr, ph = place(dr, dh)
            slot = (pr, c, ph)
            copy = far_copy(buf, slot, fwd.at[dr, dh], recv.at[slot], {"col": other_c})
            copy.wait_recv()
            copy.start()
            sent.append(copy)
        return sent

    def arrived(buf, fwd, recv):
        for dr, dh in steps:
            pr, ph = place(dr, dh)
            slot = (pr, other_c, ph)
            far_copy(buf, slot, fwd.at[dr, dh], recv.at[slot], {"col": other_c}).wait_recv()

    sent = spread(pbuf, p_send, p_fwd, p_recv)
    for load in loads[1:5]:
        load.wait()

    def weights(core, rows):
        return (pl.ds(3 * core, 3), rows)

    theirs = pl.ds(pl.multiple_of(other_h * (width // 2), width // 2), width // 2)
    w_far = far_copy(wbuf, weights(c, mine), w_send.at[0], w_recv.at[0], {"chan": other_h})
    w_far.start()
    loads[5].wait()
    pack(cot_ref, cbuf)
    sent += spread(cbuf, c_send, c_fwd, c_recv)

    loads[6].wait()
    token = lax.broadcasted_iota(jnp.int32, (n, width), 0)
    mj = jnp.zeros((n, width), f32)
    for j in range(n):
        mj = jnp.where(token == j, mask_ref[j].astype(f32), mj)
    mj_s[...] = jnp.zeros(mj_s.shape, f32)
    mj_s[0:n, :] = mj
    tail = z_s.shape[0] - n * n
    for s in (z_s, zh_s, l_s, r_s):
        s[n * n : n * n + tail, :] = jnp.zeros((tail, width), f32)

    sent += relay(pbuf, p_fwd, p_recv)
    w_near = far_copy(wbuf, weights(c, theirs), w_send.at[1], w_recv.at[1], {"col": other_c})
    far_copy(wbuf, weights(c, theirs), w_send.at[0], w_recv.at[0], {"chan": other_h}).wait_recv()
    w_near.start()
    sent += [w_far, w_near]
    arrived(pbuf, p_fwd, p_recv)
    far_copy(wbuf, weights(other_c, theirs), w_send.at[1], w_recv.at[1], {"col": other_c}).wait_recv()

    w_left = wbuf[0:2].reshape(2 * width, width)
    w_right = wbuf[3:5].reshape(2 * width, width)
    w_gate, w_out = wbuf[2], wbuf[5]

    def unpack(buf, dst, br):
        for bc in range(2):
            for part, full in enumerate(merge(buf[br, bc, 0], buf[br, bc, 1])):
                for t in range(half_rows):
                    start = (br * rows + part * half_rows + t) * n + bc * cols
                    dst[start : start + cols, :] = full[t, 0:cols, :]

    for br in range(n_row):
        unpack(pbuf, z_s, br)
        at = slice(br * block, (br + 1) * block)
        z = z_s[at, :]
        mean, rstd = norm_stats(z)
        zh = (z - mean) * rstd
        zh_s[at, :] = zh
        zn = zh.astype(bf16)
        pm = jnp.concatenate([mj * mask_ref[br * rows + t].astype(f32) for t in range(rows)], axis=0)
        proj = dot(zn, w_left, True)
        left = pm * sigmoid(proj[:, width:]) * proj[:, :width]
        l_s[at, :] = left.astype(bf16).astype(f32)
        proj = dot(zn, w_right, True)
        right = pm * sigmoid(proj[:, width:]) * proj[:, :width]
        r_s[at, :] = right.astype(bf16).astype(f32)

    sent += relay(cbuf, c_fwd, c_recv)

    def products(rows_ref, turned_ref):
        def step(k, sums):
            turned = turned_ref[pl.ds(k, n, stride=n), :]
            return tuple(
                s + rows_ref[pl.ds((r * rows + i) * n + k, 1), :] * turned
                for i, s in enumerate(sums)
            )

        sums = lax.fori_loop(0, n, step, (jnp.zeros((n, width), f32),) * rows, unroll=4)
        return jnp.concatenate(sums, axis=0)

    tri_a = products(l_s, r_s)
    tri_b = products(r_s, l_s)

    arrived(cbuf, c_fwd, c_recv)
    for br in range(n_row):
        unpack(cbuf, c_s, br)

    def turned_block(ref):
        return jnp.concatenate(
            [ref[pl.ds(r * rows + j, n, stride=n), :] for j in range(rows)], axis=0
        )

    def hidden(tri, zn, cot):
        mean, rstd = norm_stats(tri)
        xhat = (tri - mean) * rstd
        proj_out = dot(xhat.astype(bf16), w_out)
        gate = sigmoid(dot(zn, w_gate, True))
        dxn = dot((cot * gate).astype(bf16), w_out, True)
        dtri = (dxn - lane_mean(dxn) - xhat * lane_mean(dxn * xhat)) * rstd
        return proj_out, gate, dtri.astype(bf16).astype(f32)

    own_rows = pl.ds(pl.multiple_of(r * block, 8), block)
    cot_a = c_s[own_rows, :]
    proj_out, gate, dtri = hidden(tri_a, zh_s[own_rows, :].astype(bf16), cot_a)
    da_s[...] = dtri
    u_s[...] = jnp.zeros(u_s.shape, f32)
    dg_s[...] = jnp.zeros(dg_s.shape, f32)
    u_s[0:block, :] = gate * proj_out
    dg_s[0:block, :] = cot_a * proj_out * gate * (1.0 - gate)
    _, _, dtri = hidden(tri_b, turned_block(zh_s).astype(bf16), turned_block(c_s))
    db_s[...] = dtri

    def own_cells(ref, first):
        return jnp.concatenate(
            [ref[pl.ds((first + i) * n + c * cols, pad), :] for i in range(rows)], axis=0
        )

    def gradients(d_ref, other_ref):
        def step(j, sums):
            other = other_ref[pl.ds(j * n + c * cols, pad), :]
            return tuple(s + d_ref[pl.ds(i * n + j, 1), :] * other for i, s in enumerate(sums))

        sums = lax.fori_loop(0, n, step, (jnp.zeros((pad, width), f32),) * rows, unroll=4)
        return jnp.concatenate(sums, axis=0)

    dleft = gradients(da_s, r_s)
    dright = gradients(db_s, l_s)

    z = own_cells(z_s, r * rows)
    mean, rstd = norm_stats(z)
    zhat = (z - mean) * rstd
    zn = zhat.astype(bf16)
    own_mask = mj_s[pl.ds(c * cols, pad), :]
    pm = jnp.concatenate(
        [own_mask * mask_ref[r * rows + i].astype(f32) for i in range(rows)], axis=0
    )
    dzn = dot(own_cells(dg_s, 0).astype(bf16), w_gate)
    for grads, w in ((dleft, w_left), (dright, w_right)):
        proj = dot(zn, w, True)
        gated = sigmoid(proj[:, width:])
        dpre = [grads * pm * gated, grads * pm * proj[:, :width] * gated * (1.0 - gated)]
        dzn = dzn + dot(jnp.concatenate(dpre, axis=1).astype(bf16), w)
    grad = (dzn - lane_mean(dzn) - zhat * lane_mean(dzn * zhat)) * rstd

    for i, value in enumerate((own_cells(u_s, 0), grad)):
        value = jnp.where(h == 0, value, pltpu.roll(value, width // 2, 1))
        out_ref[i] = value.reshape(rows, pad, width)[:, 0:cols, 0 : width // 2].astype(bf16)
    for copy in sent:
        copy.wait_send()


def gathered(n_row, pair, token_mask, w_in, w_gate, w_out, cotangent):
    f32, bf16 = jnp.float32, jnp.bfloat16
    rows, cols, chans = pair.shape
    n = rows * n_row
    width = 2 * chans
    pad = -(-cols // 16) * 16
    vmem = pl.BlockSpec(memory_space=pltpu.VMEM)
    shards = pltpu.VMEM((n_row, 2, 2, rows // 2, pad, width), bf16)
    cells = pltpu.VMEM((n * n + 8, width), f32)
    block = pltpu.VMEM((rows * n, width), f32)
    block_and_tail = pltpu.VMEM((rows * n + 8, width), f32)
    dma = pltpu.SemaphoreType.DMA
    out = pl.pallas_call(
        functools.partial(kernel, n_row),
        out_shape=jax.ShapeDtypeStruct((2,) + pair.shape, bf16),
        in_specs=[pl.BlockSpec(memory_space=pltpu.HBM)] * 6,
        out_specs=vmem,
        scratch_shapes=[
            pltpu.VMEM(pair.shape, bf16), pltpu.VMEM(pair.shape, bf16),
            pltpu.SMEM(token_mask.shape, jnp.int32), dma((7,)),
            shards, shards, pltpu.VMEM((6, width, width), bf16),
            cells, cells, cells, cells, cells, pltpu.VMEM((n + 8, width), f32),
            block_and_tail, block_and_tail, block, block,
            dma((n_row, 2)), dma((n_row, 2)), dma((n_row, 2, 2)),
            dma((n_row, 2)), dma((n_row, 2)), dma((n_row, 2, 2)),
            dma((2,)), dma((2,)),
        ],
        compiler_params=pltpu.CompilerParams(
            collective_id=0, has_side_effects=True, vmem_limit_bytes=60 * 2**20
        ),
    )(pair, token_mask, w_in.transpose(1, 2, 0), w_gate.T, w_out, cotangent)
    return out[0], out[1]


def body(pair, token_mask, w_in, w_gate, w_out, cotangent):
    f32 = jnp.float32
    brain_float_half = jnp.bfloat16
    rows = pair.shape[0]
    cols = pair.shape[1]
    chans = pair.shape[2]
    width_c = w_in.shape[0]
    hidden_dev = w_in.shape[2]
    hidden_channel_width = hidden_dev * lax.axis_size("chan")
    row_start = lax.axis_index("row") * rows
    col_start = lax.axis_index("col") * cols
    chan_start = lax.axis_index("chan") * chans
    zfull = lax.all_gather(pair, "chan", axis=2, tiled=True).astype(f32)
    mean_z = jnp.sum(zfull, axis=-1, keepdims=True) / width_c
    square_z = jnp.sum(zfull * zfull, axis=-1, keepdims=True) / width_c
    rstd_z = lax.rsqrt(square_z - mean_z * mean_z + EPS)
    zhat = (zfull - mean_z) * rstd_z
    zn_b = zhat.astype(brain_float_half)
    proj = jnp.einsum("rkc,cqh->rkqh", zn_b, w_in, preferred_element_type=f32)
    maskf = token_mask.astype(f32)
    mask_rows = lax.dynamic_slice_in_dim(maskf, row_start, rows)
    mask_cols = lax.dynamic_slice_in_dim(maskf, col_start, cols)
    pmask = (mask_rows[:, None] * mask_cols[None, :])[..., None]
    sig_one = jax.nn.sigmoid(proj[:, :, 1])
    sig_three = jax.nn.sigmoid(proj[:, :, 3])
    left = (pmask * sig_one * proj[:, :, 0]).astype(brain_float_half)
    right = (pmask * sig_three * proj[:, :, 2]).astype(brain_float_half)
    partial_tri = jnp.einsum(
        "ikh,jkh->ijh",
        left,
        lax.all_gather(right, "row", axis=0, tiled=True),
        preferred_element_type=f32,
    )
    triangle_product = lax.psum_scatter(partial_tri, "col", scatter_dimension=1, tiled=True)
    sum_x, square_x = lax.psum(
        (jnp.sum(triangle_product, axis=-1), jnp.sum(triangle_product * triangle_product, axis=-1)),
        "chan",
    )
    input_mean = (sum_x / hidden_channel_width)[..., None]
    input_inverse_deviation = lax.rsqrt(
        square_x[..., None] / hidden_channel_width - input_mean * input_mean + EPS
    )
    centered_input = (triangle_product - input_mean) * input_inverse_deviation
    normed_input_low_precision = centered_input.astype(brain_float_half)
    out_term = jnp.einsum(
        "rch,hd->rcd", normed_input_low_precision, w_out, preferred_element_type=f32
    )
    proj_out = lax.psum_scatter(out_term, "chan", scatter_dimension=2, tiled=True)
    gate = jax.nn.sigmoid(jnp.einsum("rcd,de->rce", zn_b, w_gate, preferred_element_type=f32))
    update = (gate * proj_out).astype(brain_float_half)
    cot = cotangent.astype(f32)
    dproj = (cot * gate).astype(brain_float_half)
    dgate = (cot * proj_out * gate * (1.0 - gate)).astype(brain_float_half)
    dproj_all = lax.all_gather(dproj, "chan", axis=2, tiled=True)
    normed_input_gradient = jnp.einsum("rcd,hd->rch", dproj_all, w_out, preferred_element_type=f32)
    first_operand, second_operand = lax.psum(
        (
            jnp.sum(normed_input_gradient, axis=-1),
            jnp.sum(normed_input_gradient * centered_input, axis=-1),
        ),
        "chan",
    )
    triangle_gradient = (
        (
            normed_input_gradient
            - (first_operand / hidden_channel_width)[..., None]
            - centered_input * (second_operand / hidden_channel_width)[..., None]
        )
        * input_inverse_deviation
    ).astype(brain_float_half)
    dtri_rows = lax.all_gather(triangle_gradient, "col", axis=1, tiled=True)
    block = dtri_rows
    dleft = jnp.einsum(
        "ijh,jkh->ikh",
        block,
        lax.all_gather(right, "row", axis=0, tiled=True),
        preferred_element_type=f32,
    )
    dtri_turned = lax.all_to_all(dtri_rows, "row", split_axis=1, concat_axis=0, tiled=True)
    block = dtri_turned
    dright = jnp.einsum(
        "ijh,ikh->jkh",
        block,
        lax.all_gather(left, "row", axis=0, tiled=True),
        preferred_element_type=f32,
    )
    dpre = jnp.stack(
        [
            dleft * pmask * sig_one,
            dleft * pmask * proj[:, :, 0] * sig_one * (1.0 - sig_one),
            dright * pmask * sig_three,
            dright * pmask * proj[:, :, 2] * sig_three * (1.0 - sig_three),
        ],
        axis=2,
    ).astype(brain_float_half)
    dzn_term = jnp.einsum("rkqh,cqh->rkc", dpre, w_in, preferred_element_type=f32)
    dzn_term = dzn_term + jnp.einsum("rkd,cd->rkc", dgate, w_gate, preferred_element_type=f32)
    dzn = lax.psum_scatter(dzn_term, "chan", scatter_dimension=2, tiled=True)
    zhat_own = lax.dynamic_slice_in_dim(zhat, chan_start, chans, 2)
    first_z, second_z = lax.psum((jnp.sum(dzn, axis=-1), jnp.sum(dzn * zhat_own, axis=-1)), "chan")
    pair_grad = (
        (dzn - (first_z / width_c)[..., None] - zhat_own * (second_z / width_c)[..., None]) * rstd_z
    ).astype(brain_float_half)
    return (update, pair_grad)


def plan(pair, token_mask, w_in, w_gate, w_out, cotangent):
    n_row, n_col, n_chan = (lax.axis_size(a) for a in ("row", "col", "chan"))
    rows, cols, chans = pair.shape
    n = token_mask.shape[0]
    small = n <= 32 and n % 8 == 0 and rows % 2 == 0 and cols % 4 == 0 and rows * n % 16 == 0
    shaped = n_col == 2 and n_chan == 2 and chans == 64 and w_in.shape == (128, 4, 64)
    if small and shaped and -(-cols // 16) * 16 - cols <= 8:
        return gathered(n_row, pair, token_mask, w_in, w_gate, w_out, cotangent)
    return body(pair, token_mask, w_in, w_gate, w_out, cotangent)


def solution(mesh):
    return jax.shard_map(
        plan,
        mesh=mesh,
        in_specs=(
            P(("groups", "row"), "col", "chan"),
            P("groups"),
            P(None, None, "chan"),
            P(None, "chan"),
            P("chan", None),
            P(("groups", "row"), "col", "chan"),
        ),
        out_specs=(P(("groups", "row"), "col", "chan"), P(("groups", "row"), "col", "chan")),
        check_vma=False,
    )
```

```python
import functools

import jax
import jax.numpy as jnp
from jax import lax
from jax.experimental import pallas as pl
from jax.experimental.pallas import tpu as pltpu
from jax.sharding import PartitionSpec as P

EPS = 1e-05
MESH = pl.DeviceIdType.MESH


def sigmoid(x):
    return 1.0 / (1.0 + jnp.exp(-x))


def lane_mean(x):
    return jnp.sum(x, axis=-1, keepdims=True) * (1.0 / x.shape[-1])


def norm_stats(x):
    mean = lane_mean(x)
    return mean, lax.rsqrt(lane_mean(x * x) - mean * mean + EPS)


def merge(first, second):
    first, second = first.astype(jnp.float32), second.astype(jnp.float32)
    axis = first.ndim - 1
    width = first.shape[-1]
    low = lax.broadcasted_iota(jnp.int32, first.shape, axis) < width // 2
    return (
        jnp.where(low, first, pltpu.roll(second, width // 2, axis)),
        jnp.where(low, pltpu.roll(first, width // 2, axis), second),
    )


def dot(a, b, transposed=False):
    return lax.dot_general(
        a, b, (((1,), (1 if transposed else 0,)), ((), ())), preferred_element_type=jnp.float32
    )


def kernel(
    n_row, pair_hbm, mask_hbm, w_in_hbm, w_gate_hbm, w_out_hbm, cot_hbm, out_ref,
    pair_ref, cot_ref, mask_ref, in_sem, pbuf, cbuf, wbuf, z_s, zh_s, c_s, l_s, r_s, mj_s, u_s, dg_s, da_s, db_s,
    p_send, p_fwd, p_recv, c_send, c_fwd, c_recv, w_send, w_recv,
):
    f32, bf16 = jnp.float32, jnp.bfloat16
    rows, cols, _ = pair_ref.shape
    n = rows * n_row
    width = 2 * pair_ref.shape[2]
    half_rows = rows // 2
    pad = pbuf.shape[4]
    block = rows * n
    r, c, h = lax.axis_index("row"), lax.axis_index("col"), lax.axis_index("chan")
    other_c, other_h = 1 - c, 1 - h
    wanted_c = lax.div(r * rows, cols)
    plane = [(0, 1), (1, 0), (1, 1)]

    def partner(dc, dh):
        return lax.rem(c + dc, 2), lax.rem(h + dh, 2)


    def place(dr, dh):
        return lax.rem(r + dr, n_row), lax.rem(h + dh, 2)

    steps = [(dr, dh) for dr in range(n_row) for dh in range(2)]
    far = [s for s in steps if s != (0, 0)]

    mine = pl.ds(pl.multiple_of(h * (width // 2), width // 2), width // 2)
    loads = [
        pltpu.make_async_copy(src, dst, in_sem.at[i])
        for i, (src, dst) in enumerate(
            [
                (pair_hbm, pair_ref),
                (w_in_hbm.at[0:2], wbuf.at[0:2, mine]),
                (w_gate_hbm, wbuf.at[2, mine]),
                (w_in_hbm.at[2:4], wbuf.at[3:5, mine]),
                (w_out_hbm, wbuf.at[5, mine]),
                (cot_hbm, cot_ref),
                (mask_hbm, mask_ref),
            ]
        )
    ]
    for load in loads:
        load.start()

    barrier = pltpu.get_barrier_semaphore()
    everyone = [(dr, 0, dh) for dr, dh in far] + [(0, 1, 0)]
    for dr, dc, dh in everyone:
        pc, ph = partner(dc, dh)
        device = {"row": lax.rem(r + dr, n_row), "col": pc, "chan": ph}
        pl.semaphore_signal(barrier, inc=1, device_id=device, device_id_type=MESH)

    def pack(ref, buf):
        x = ref[...].astype(f32)
        x = jnp.concatenate([x[:half_rows], x[half_rows:]], axis=-1)
        buf[r, c, h] = jnp.zeros(buf.shape[3:], bf16)
        buf[r, c, h, :, 0:cols, :] = x.astype(bf16)

    loads[0].wait()
    pack(pair_ref, pbuf)
    pl.semaphore_wait(barrier, len(everyone))

    def far_copy(buf, slot, send, recv, device):
        return pltpu.make_async_remote_copy(
            src_ref=buf.at[slot], dst_ref=buf.at[slot], send_sem=send, recv_sem=recv,
            device_id=device, device_id_type=MESH,
        )

    def spread(buf, send, fwd, recv):
        sent = []
        own = (r, c, h)
        for dr, dh in far:
            pr, ph = place(dr, dh)
            sent.append(
                far_copy(buf, own, send.at[dr, dh], recv.at[own], {"row": pr, "chan": ph})
            )
        sent.append(far_copy(buf, own, fwd.at[0, 0], recv.at[own], {"col": other_c}))
        for copy in sent:
            copy.start()
        return sent

    def relay(buf, fwd, recv, dr):
        for dh in range(2):
            if (dr, dh) == (0, 0):
                continue
            pr, ph = place(dr, dh)
            slot = (pr, c, ph)
            copy = far_copy(buf, slot, fwd.at[dr, dh], recv.at[slot], {"col": other_c})
            copy.wait_recv()
            copy.start()
            sent.append(copy)

    def wait_for(buf, recv, slot):
        far_copy(buf, slot, w_send.at[0], recv.at[slot], {"col": other_c}).wait_recv()

    def cot_copies(act):
        own = (r, c, h)
        for dr in range(n_row):
            pr = lax.rem(r + dr, n_row)

            def to_plane():
                for dc, dh in [(0, 0), (0, 1)] if dr else [(0, 1), (1, 0)]:
                    pc, ph = partner(dc, dh)
                    device = {"row": pr, "col": pc, "chan": ph}
                    act(far_copy(cbuf, own, c_send.at[dr, dc, dh], c_recv.at[own], device))

            if dr:
                pl.when(lax.div(pr * rows, cols) == c)(to_plane)
            else:
                to_plane()

    def cot_relay(act):
        def pass_on(dr, dh):
            slot = (lax.rem(r + dr, n_row), c, lax.rem(h + dh, 2))
            act(far_copy(cbuf, slot, c_fwd.at[dr, dh], c_recv.at[slot], {"col": other_c}))

        pass_on(0, 1)

        @pl.when(c == wanted_c)
        def _():
            for dr in range(1, n_row):
                for dh in range(2):
                    pass_on(dr, dh)

    sent = spread(pbuf, p_send, p_fwd, p_recv)
    for load in loads[1:5]:
        load.wait()

    def weights(core, rows):
        return (pl.ds(3 * core, 3), rows)

    theirs = pl.ds(pl.multiple_of(other_h * (width // 2), width // 2), width // 2)
    w_far = far_copy(wbuf, weights(c, mine), w_send.at[0], w_recv.at[0], {"chan": other_h})
    w_far.start()
    loads[5].wait()
    pack(cot_ref, cbuf)
    cot_copies(lambda copy: copy.start())

    loads[6].wait()
    token = lax.broadcasted_iota(jnp.int32, (n, width), 0)
    mj = jnp.zeros((n, width), f32)
    for j in range(n):
        mj = jnp.where(token == j, mask_ref[j].astype(f32), mj)
    mj_s[...] = jnp.zeros(mj_s.shape, f32)
    mj_s[0:n, :] = mj
    tail = z_s.shape[0] - n * n
    for s in (z_s, zh_s, l_s, r_s):
        s[n * n : n * n + tail, :] = jnp.zeros((tail, width), f32)

    relay(pbuf, p_fwd, p_recv, 0)
    w_near = far_copy(wbuf, weights(c, theirs), w_send.at[1], w_recv.at[1], {"col": other_c})
    far_copy(wbuf, weights(c, theirs), w_send.at[0], w_recv.at[0], {"chan": other_h}).wait_recv()
    w_near.start()
    sent += [w_far, w_near]
    for dr in range(1, n_row):
        relay(pbuf, p_fwd, p_recv, dr)
    far_copy(wbuf, weights(other_c, theirs), w_send.at[1], w_recv.at[1], {"col": other_c}).wait_recv()

    w_left = wbuf[0:2].reshape(2 * width, width)
    w_right = wbuf[3:5].reshape(2 * width, width)
    w_gate, w_out = wbuf[2], wbuf[5]

    def unpack(buf, dst, br, bc):
        for part, full in enumerate(merge(buf[br, bc, 0], buf[br, bc, 1])):
            for t in range(half_rows):
                first = pl.multiple_of(br * block, 8) + (part * half_rows + t) * n + bc * cols
                dst[pl.ds(first, cols), :] = full[t, 0:cols, :]

    for dr in range(n_row):
        br = lax.rem(r + dr, n_row)
        for dh in range(2):
            wait_for(pbuf, p_recv, (br, other_c, lax.rem(h + dh, 2)))
        for bc in range(2):
            unpack(pbuf, z_s, br, bc)
        at = pl.ds(pl.multiple_of(br * block, 8), block)
        z = z_s[at, :]
        mean, rstd = norm_stats(z)
        zh = (z - mean) * rstd
        zh_s[at, :] = zh
        zn = zh.astype(bf16)
        pm = jnp.concatenate([mj * mask_ref[br * rows + t].astype(f32) for t in range(rows)], axis=0)
        proj = dot(zn, w_left, True)
        left = pm * sigmoid(proj[:, width:]) * proj[:, :width]
        l_s[at, :] = left.astype(bf16).astype(f32)
        proj = dot(zn, w_right, True)
        right = pm * sigmoid(proj[:, width:]) * proj[:, :width]
        r_s[at, :] = right.astype(bf16).astype(f32)

    def received_and_passed(copy):
        copy.wait_recv()
        copy.start()

    cot_relay(received_and_passed)

    def products(step, start):
        sums = lax.fori_loop(0, n, step, ((start,) * rows,) * 2, unroll=24)
        return [jnp.concatenate(s, axis=0) for s in sums]

    def tri_step(k, sums):
        out = []
        for rows_ref, turned_ref, parts in ((l_s, r_s, sums[0]), (r_s, l_s, sums[1])):
            turned = turned_ref[pl.ds(k, n, stride=n), :]
            out.append(tuple(
                s + rows_ref[pl.ds((r * rows + i) * n + k, 1), :] * turned
                for i, s in enumerate(parts)
            ))
        return tuple(out)

    tri_a, tri_b = products(tri_step, jnp.zeros((n, width), f32))

    def turned_block(ref):
        return jnp.concatenate(
            [ref[pl.ds(r * rows + j, n, stride=n), :] for j in range(rows)], axis=0
        )

    def own_cells(ref, first):
        return jnp.concatenate(
            [ref[pl.ds((first + i) * n + c * cols, pad), :] for i in range(rows)], axis=0
        )

    def forward(tri, zn):
        mean, rstd = norm_stats(tri)
        xhat = (tri - mean) * rstd
        proj_out = dot(xhat.astype(bf16), w_out)
        gate = sigmoid(dot(zn, w_gate, True))
        return xhat, rstd, proj_out, gate

    def backward(xhat, rstd, gate, cot):
        dxn = dot((cot * gate).astype(bf16), w_out, True)
        dtri = (dxn - lane_mean(dxn) - xhat * lane_mean(dxn * xhat)) * rstd
        return dtri.astype(bf16).astype(f32)

    own_rows = pl.ds(pl.multiple_of(r * block, 8), block)
    xhat_a, rstd_a, proj_out, gate_a = forward(tri_a, zh_s[own_rows, :].astype(bf16))
    xhat_b, rstd_b, _, gate_b = forward(tri_b, turned_block(zh_s).astype(bf16))
    u_s[0:block, :] = gate_a * proj_out
    u_s[block:, :] = jnp.zeros((u_s.shape[0] - block, width), f32)
    dg_s[block:, :] = jnp.zeros((u_s.shape[0] - block, width), f32)

    z = own_cells(z_s, r * rows)
    mean, rstd = norm_stats(z)
    zhat = (z - mean) * rstd
    zn = zhat.astype(bf16)
    own_mask = mj_s[pl.ds(c * cols, pad), :]
    pm = jnp.concatenate(
        [own_mask * mask_ref[r * rows + i].astype(f32) for i in range(rows)], axis=0
    )
    factors = []
    for w in (w_left, w_right):
        proj = dot(zn, w, True)
        gated = pm * sigmoid(proj[:, width:])
        factors.append((gated, proj[:, :width] * gated * (1.0 - gated)))

    def put(i, value):
        value = jnp.where(h == 0, value, pltpu.roll(value, width // 2, 1))
        out_ref[i] = value.reshape(rows, pad, width)[:, 0:cols, 0 : width // 2].astype(bf16)

    put(0, own_cells(u_s, 0))

    for bh in range(2):
        wait_for(cbuf, c_recv, (r, other_c, bh))
    for bc in range(2):
        unpack(cbuf, c_s, r, bc)
    for dr in range(1, n_row):
        br = lax.rem(r + dr, n_row)
        for bh in range(2):
            slot = (br, wanted_c, bh)
            pl.when(c != wanted_c)(functools.partial(wait_for, cbuf, c_recv, slot))
        unpack(cbuf, c_s, br, wanted_c)

    cot_a = c_s[own_rows, :]
    dg_s[0:block, :] = cot_a * proj_out * gate_a * (1.0 - gate_a)
    da_s[...] = backward(xhat_a, rstd_a, gate_a, cot_a)
    db_s[...] = backward(xhat_b, rstd_b, gate_b, turned_block(c_s))

    def gradient_step(j, sums):
        out = []
        for d_ref, other_ref, parts in ((da_s, r_s, sums[0]), (db_s, l_s, sums[1])):
            other = other_ref[pl.ds(j * n + c * cols, pad), :]
            out.append(tuple(
                s + d_ref[pl.ds(i * n + j, 1), :] * other for i, s in enumerate(parts)
            ))
        return tuple(out)

    grads = products(gradient_step, jnp.zeros((pad, width), f32))
    dzn = dot(own_cells(dg_s, 0).astype(bf16), w_gate)
    for grad, (value, gate), w in zip(grads, factors, (w_left, w_right)):
        dzn = dzn + dot(jnp.concatenate([grad * value, grad * gate], axis=1).astype(bf16), w)
    put(1, (dzn - lane_mean(dzn) - zhat * lane_mean(dzn * zhat)) * rstd)
    for copy in sent:
        copy.wait_send()
    cot_copies(lambda copy: copy.wait_send())
    cot_relay(lambda copy: copy.wait_send())


def gathered(n_row, pair, token_mask, w_in, w_gate, w_out, cotangent):
    f32, bf16 = jnp.float32, jnp.bfloat16
    rows, cols, chans = pair.shape
    n = rows * n_row
    width = 2 * chans
    pad = -(-cols // 16) * 16
    vmem = pl.BlockSpec(memory_space=pltpu.VMEM)
    shards = pltpu.VMEM((n_row, 2, 2, rows // 2, pad, width), bf16)
    cells = pltpu.VMEM((n * n + 8, width), f32)
    block = pltpu.VMEM((rows * n, width), f32)
    block_and_tail = pltpu.VMEM((rows * n + 8, width), f32)
    dma = pltpu.SemaphoreType.DMA
    args = (pair, token_mask, w_in.transpose(1, 2, 0), w_gate.T, w_out, cotangent)
    args = [pltpu.with_memory_space_constraint(a, pltpu.HBM) for a in args]
    out = pl.pallas_call(
        functools.partial(kernel, n_row),
        out_shape=pltpu.VMEM((2,) + pair.shape, bf16),
        in_specs=[pl.BlockSpec(memory_space=pltpu.HBM)] * 6,
        out_specs=vmem,
        scratch_shapes=[
            pltpu.VMEM(pair.shape, bf16), pltpu.VMEM(pair.shape, bf16),
            pltpu.SMEM(token_mask.shape, jnp.int32), dma((7,)),
            shards, shards, pltpu.VMEM((6, width, width), bf16),
            cells, cells, cells, cells, cells, pltpu.VMEM((n + 8, width), f32),
            block_and_tail, block_and_tail, block, block,
            dma((n_row, 2)), dma((n_row, 2)), dma((n_row, 2, 2)),
            dma((n_row, 2, 2)), dma((n_row, 2)), dma((n_row, 2, 2)),
            dma((2,)), dma((2,)),
        ],
        compiler_params=pltpu.CompilerParams(
            collective_id=0, has_side_effects=True, vmem_limit_bytes=24 * 2**20
        ),
    )(*args)
    return out[0], out[1]


def body(pair, token_mask, w_in, w_gate, w_out, cotangent):
    f32 = jnp.float32
    brain_float_half = jnp.bfloat16
    rows = pair.shape[0]
    cols = pair.shape[1]
    chans = pair.shape[2]
    width_c = w_in.shape[0]
    hidden_dev = w_in.shape[2]
    hidden_channel_width = hidden_dev * lax.axis_size("chan")
    row_start = lax.axis_index("row") * rows
    col_start = lax.axis_index("col") * cols
    chan_start = lax.axis_index("chan") * chans
    zfull = lax.all_gather(pair, "chan", axis=2, tiled=True).astype(f32)
    mean_z = jnp.sum(zfull, axis=-1, keepdims=True) / width_c
    square_z = jnp.sum(zfull * zfull, axis=-1, keepdims=True) / width_c
    rstd_z = lax.rsqrt(square_z - mean_z * mean_z + EPS)
    zhat = (zfull - mean_z) * rstd_z
    zn_b = zhat.astype(brain_float_half)
    proj = jnp.einsum("rkc,cqh->rkqh", zn_b, w_in, preferred_element_type=f32)
    maskf = token_mask.astype(f32)
    mask_rows = lax.dynamic_slice_in_dim(maskf, row_start, rows)
    mask_cols = lax.dynamic_slice_in_dim(maskf, col_start, cols)
    pmask = (mask_rows[:, None] * mask_cols[None, :])[..., None]
    sig_one = jax.nn.sigmoid(proj[:, :, 1])
    sig_three = jax.nn.sigmoid(proj[:, :, 3])
    left = (pmask * sig_one * proj[:, :, 0]).astype(brain_float_half)
    right = (pmask * sig_three * proj[:, :, 2]).astype(brain_float_half)
    partial_tri = jnp.einsum(
        "ikh,jkh->ijh",
        left,
        lax.all_gather(right, "row", axis=0, tiled=True),
        preferred_element_type=f32,
    )
    triangle_product = lax.psum_scatter(partial_tri, "col", scatter_dimension=1, tiled=True)
    sum_x, square_x = lax.psum(
        (jnp.sum(triangle_product, axis=-1), jnp.sum(triangle_product * triangle_product, axis=-1)),
        "chan",
    )
    input_mean = (sum_x / hidden_channel_width)[..., None]
    input_inverse_deviation = lax.rsqrt(
        square_x[..., None] / hidden_channel_width - input_mean * input_mean + EPS
    )
    centered_input = (triangle_product - input_mean) * input_inverse_deviation
    normed_input_low_precision = centered_input.astype(brain_float_half)
    out_term = jnp.einsum(
        "rch,hd->rcd", normed_input_low_precision, w_out, preferred_element_type=f32
    )
    proj_out = lax.psum_scatter(out_term, "chan", scatter_dimension=2, tiled=True)
    gate = jax.nn.sigmoid(jnp.einsum("rcd,de->rce", zn_b, w_gate, preferred_element_type=f32))
    update = (gate * proj_out).astype(brain_float_half)
    cot = cotangent.astype(f32)
    dproj = (cot * gate).astype(brain_float_half)
    dgate = (cot * proj_out * gate * (1.0 - gate)).astype(brain_float_half)
    dproj_all = lax.all_gather(dproj, "chan", axis=2, tiled=True)
    normed_input_gradient = jnp.einsum("rcd,hd->rch", dproj_all, w_out, preferred_element_type=f32)
    first_operand, second_operand = lax.psum(
        (
            jnp.sum(normed_input_gradient, axis=-1),
            jnp.sum(normed_input_gradient * centered_input, axis=-1),
        ),
        "chan",
    )
    triangle_gradient = (
        (
            normed_input_gradient
            - (first_operand / hidden_channel_width)[..., None]
            - centered_input * (second_operand / hidden_channel_width)[..., None]
        )
        * input_inverse_deviation
    ).astype(brain_float_half)
    dtri_rows = lax.all_gather(triangle_gradient, "col", axis=1, tiled=True)
    block = dtri_rows
    dleft = jnp.einsum(
        "ijh,jkh->ikh",
        block,
        lax.all_gather(right, "row", axis=0, tiled=True),
        preferred_element_type=f32,
    )
    dtri_turned = lax.all_to_all(dtri_rows, "row", split_axis=1, concat_axis=0, tiled=True)
    block = dtri_turned
    dright = jnp.einsum(
        "ijh,ikh->jkh",
        block,
        lax.all_gather(left, "row", axis=0, tiled=True),
        preferred_element_type=f32,
    )
    dpre = jnp.stack(
        [
            dleft * pmask * sig_one,
            dleft * pmask * proj[:, :, 0] * sig_one * (1.0 - sig_one),
            dright * pmask * sig_three,
            dright * pmask * proj[:, :, 2] * sig_three * (1.0 - sig_three),
        ],
        axis=2,
    ).astype(brain_float_half)
    dzn_term = jnp.einsum("rkqh,cqh->rkc", dpre, w_in, preferred_element_type=f32)
    dzn_term = dzn_term + jnp.einsum("rkd,cd->rkc", dgate, w_gate, preferred_element_type=f32)
    dzn = lax.psum_scatter(dzn_term, "chan", scatter_dimension=2, tiled=True)
    zhat_own = lax.dynamic_slice_in_dim(zhat, chan_start, chans, 2)
    first_z, second_z = lax.psum((jnp.sum(dzn, axis=-1), jnp.sum(dzn * zhat_own, axis=-1)), "chan")
    pair_grad = (
        (dzn - (first_z / width_c)[..., None] - zhat_own * (second_z / width_c)[..., None]) * rstd_z
    ).astype(brain_float_half)
    return (update, pair_grad)


def plan(pair, token_mask, w_in, w_gate, w_out, cotangent):
    n_row, n_col, n_chan = (lax.axis_size(a) for a in ("row", "col", "chan"))
    rows, cols, chans = pair.shape
    n = token_mask.shape[0]
    small = n <= 32 and n % 8 == 0 and rows % 2 == 0 and cols % 4 == 0 and rows * n % 16 == 0
    small = small and cols % rows == 0
    shaped = n_col == 2 and n_chan == 2 and chans == 64 and w_in.shape == (128, 4, 64)
    if small and shaped and -(-cols // 16) * 16 - cols <= 8:
        return gathered(n_row, pair, token_mask, w_in, w_gate, w_out, cotangent)
    return body(pair, token_mask, w_in, w_gate, w_out, cotangent)


def solution(mesh):
    return jax.shard_map(
        plan,
        mesh=mesh,
        in_specs=(
            P(("groups", "row"), "col", "chan"),
            P("groups"),
            P(None, None, "chan"),
            P(None, "chan"),
            P("chan", None),
            P(("groups", "row"), "col", "chan"),
        ),
        out_specs=(P(("groups", "row"), "col", "chan"), P(("groups", "row"), "col", "chan")),
        check_vma=False,
    )
```

```python
import functools

import jax
import jax.numpy as jnp
from jax import lax
from jax.experimental import pallas as pl
from jax.experimental.pallas import tpu as pltpu
from jax.sharding import PartitionSpec as P

EPS = 1e-05
MESH = pl.DeviceIdType.MESH


def sigmoid(x):
    return 1.0 / (1.0 + jnp.exp(-x))


def lane_mean(x):
    return jnp.sum(x, axis=-1, keepdims=True) * (1.0 / x.shape[-1])


def norm_stats(x):
    mean = lane_mean(x)
    return mean, lax.rsqrt(lane_mean(x * x) - mean * mean + EPS)


def merge(first, second):
    first, second = first.astype(jnp.float32), second.astype(jnp.float32)
    axis = first.ndim - 1
    width = first.shape[-1]
    low = lax.broadcasted_iota(jnp.int32, first.shape, axis) < width // 2
    return (
        jnp.where(low, first, pltpu.roll(second, width // 2, axis)),
        jnp.where(low, pltpu.roll(first, width // 2, axis), second),
    )


def dot(a, b, transposed=False):
    return lax.dot_general(
        a, b, (((1,), (1 if transposed else 0,)), ((), ())), preferred_element_type=jnp.float32
    )


def kernel(
    n_row, pair_hbm, mask_hbm, w_in_hbm, w_gate_hbm, w_out_hbm, cot_hbm, out_ref,
    pair_ref, cot_ref, mask_ref, in_sem, pbuf, cbuf, obuf, wbuf, pp_s, cp_s, z_s, zh_s, ca_s, cb_s, l_s, r_s, mj_s, u_s, dg_s, da_s, db_s,
    p_send, p_recv, p_fwd, p_near, c_send, c_recv, c_fwd, c_near, w_send, w_recv,
):
    f32, bf16 = jnp.float32, jnp.bfloat16
    rows, cols, _ = pair_ref.shape
    n = rows * n_row
    width = 2 * pair_ref.shape[2]
    half_rows = rows // 2
    pad = -(-cols // 16) * 16
    pieces = cols // rows
    block = rows * n
    r, c, h = lax.axis_index("row"), lax.axis_index("col"), lax.axis_index("chan")
    other_c, other_h = 1 - c, 1 - h
    wanted_c = lax.div(r * rows, cols)
    wanted_piece = r - wanted_c * (cols // rows)
    plane = [(0, 1), (1, 0), (1, 1)]

    def partner(dc, dh):
        return lax.rem(c + dc, 2), lax.rem(h + dh, 2)


    def place(dr, dh):
        return lax.rem(r + dr, n_row), lax.rem(h + dh, 2)

    steps = [(dr, dh) for dr in range(n_row) for dh in range(2)]
    far = [s for s in steps if s != (0, 0)]

    mine = pl.ds(pl.multiple_of(h * (width // 2), width // 2), width // 2)
    loads = [
        pltpu.make_async_copy(src, dst, in_sem.at[i])
        for i, (src, dst) in enumerate(
            [
                (pair_hbm, pair_ref),
                (w_in_hbm.at[0:2], wbuf.at[0:2, mine]),
                (w_gate_hbm, wbuf.at[2, mine]),
                (w_in_hbm.at[2:4], wbuf.at[3:5, mine]),
                (w_out_hbm, wbuf.at[5, mine]),
                (cot_hbm, cot_ref),
                (mask_hbm, mask_ref),
            ]
        )
    ]
    for load in loads:
        load.start()

    barrier = pltpu.get_barrier_semaphore()
    everyone = [(dr, 0, dh) for dr, dh in far] + [(0, 1, 0)]
    for dr, dc, dh in everyone:
        pc, ph = partner(dc, dh)
        device = {"row": lax.rem(r + dr, n_row), "col": pc, "chan": ph}
        pl.semaphore_signal(barrier, inc=1, device_id=device, device_id_type=MESH)

    def packed(ref):
        x = ref[...].astype(f32)
        return jnp.concatenate([x[:half_rows], x[half_rows:]], axis=-1)

    def pack_pair():
        x = packed(pair_ref)
        for t in range(half_rows):
            pp_s[t * cols : (t + 1) * cols, :] = x[t]
        pbuf[r, c, h] = pp_s[...].astype(bf16)

    def pack_cot():
        x = packed(cot_ref)
        for piece in range(pieces):
            for t in range(half_rows):
                cp_s[piece, t * rows : (t + 1) * rows, :] = x[t, piece * rows : (piece + 1) * rows]
            cbuf[r, c, h, piece] = cp_s[piece].astype(bf16)

    loads[0].wait()
    pack_pair()

    def far_copy(buf, slot, send, recv, device):
        part = buf.at[slot] if slot else buf
        return pltpu.make_async_remote_copy(
            src_ref=part, dst_ref=part, send_sem=send, recv_sem=recv,
            device_id=device, device_id_type=MESH,
        )

    def shard_copy(dr, dh):
        pr, ph = place(dr, dh)
        return far_copy(pbuf, (r, c, h), p_send.at[dr, dh], p_recv.at[r, h], {"row": pr, "chan": ph})

    def relay(dr):
        pr = lax.rem(r + dr, n_row)
        for dh in range(2):
            if (dr, dh) != (0, 0):
                ph = lax.rem(h + dh, 2)
                far_copy(pbuf, (pr, c, ph), p_send.at[dr, dh], p_recv.at[pr, ph], {"chan": ph}).wait_recv()
        return far_copy(pbuf, (pr, c), p_fwd.at[dr], p_near.at[dr], {"col": other_c})

    def cot_copies(act):
        act(far_copy(cbuf, (r, c, h), c_send.at[0, 1], c_recv.at[r, h], {"chan": other_h}))
        for dr in range(1, n_row):
            pr = lax.rem(r + dr, n_row)

            def to_row():
                for dh in range(2):
                    act(pltpu.make_async_remote_copy(
                        src_ref=cbuf.at[r, c, h, pr - c * pieces], dst_ref=obuf.at[r, h],
                        send_sem=c_send.at[dr, dh], recv_sem=c_recv.at[r, h],
                        device_id={"row": pr, "chan": lax.rem(h + dh, 2)}, device_id_type=MESH,
                    ))

            pl.when(lax.div(pr * rows, cols) == c)(to_row)

    def cot_relay(act, arrive):
        if arrive:
            far_copy(cbuf, (r, c, other_h), c_send.at[0, 1], c_recv.at[r, other_h], {"chan": other_h}).wait_recv()
        act(far_copy(cbuf, (r, c), c_fwd.at[0], c_near.at[0], {"col": other_c}))

        @pl.when(c == wanted_c)
        def _():
            if arrive:
                for dr in range(1, n_row):
                    pr = lax.rem(r + dr, n_row)
                    for ph in range(2):
                        far_copy(obuf, (pr, ph), c_send.at[0, 1], c_recv.at[pr, ph], {"chan": other_h}).wait_recv()
            act(far_copy(obuf, (), c_fwd.at[1], c_near.at[1], {"col": other_c}))

    def start(copy):
        copy.start()

    loads[5].wait()
    pack_cot()

    loads[6].wait()
    token = lax.broadcasted_iota(jnp.int32, (n, width), 0)
    mj = jnp.zeros((n, width), f32)
    for j in range(n):
        mj = jnp.where(token == j, mask_ref[j].astype(f32), mj)
    mj_s[...] = jnp.zeros(mj_s.shape, f32)
    mj_s[0:n, :] = mj
    tail = z_s.shape[0] - n * n
    for s in (z_s, zh_s, l_s, r_s):
        s[n * n : n * n + tail, :] = jnp.zeros((tail, width), f32)
    obuf[r] = jnp.zeros(obuf.shape[1:], bf16)
    for load in loads[1:5]:
        load.wait()
    pl.semaphore_wait(barrier, len(everyone))
    sent = [shard_copy(dr, dh) for dr, dh in far]
    for copy in sent:
        copy.start()

    def weights(core, rows):
        return (pl.ds(3 * core, 3), rows)

    theirs = pl.ds(pl.multiple_of(other_h * (width // 2), width // 2), width // 2)
    w_far = far_copy(wbuf, weights(c, mine), w_send.at[0], w_recv.at[0], {"chan": other_h})
    w_far.start()
    cot_copies(start)
    sent.append(relay(0))
    sent[-1].start()
    w_near = far_copy(wbuf, weights(c, theirs), w_send.at[1], w_recv.at[1], {"col": other_c})
    far_copy(wbuf, weights(c, theirs), w_send.at[0], w_recv.at[0], {"chan": other_h}).wait_recv()
    w_near.start()
    sent += [w_far, w_near]
    for dr in range(1, n_row):
        sent.append(relay(dr))
        sent[-1].start()
    far_copy(wbuf, weights(other_c, theirs), w_send.at[1], w_recv.at[1], {"col": other_c}).wait_recv()

    w_left = wbuf[0:2].reshape(2 * width, width)
    w_right = wbuf[3:5].reshape(2 * width, width)
    w_gate, w_out = wbuf[2], wbuf[5]

    def unpack_pair(br, bc):
        for part, full in enumerate(merge(pbuf[br, bc, 0], pbuf[br, bc, 1])):
            for t in range(half_rows):
                first = pl.multiple_of(br * block, 8) + (part * half_rows + t) * n + bc * cols
                z_s[pl.ds(first, cols), :] = full[t * cols : (t + 1) * cols]

    for dr in range(n_row):
        slot = (lax.rem(r + dr, n_row), other_c)
        far_copy(pbuf, slot, p_fwd.at[dr], p_near.at[dr], {"col": other_c}).wait_recv()
    for br in range(n_row):
        for bc in range(2):
            unpack_pair(br, bc)
    z = z_s[0 : n * n, :]
    mean, rstd = norm_stats(z)
    zh = (z - mean) * rstd
    zh_s[0 : n * n, :] = zh
    zn = zh.astype(bf16)
    for w, dst in ((w_left, l_s), (w_right, r_s)):
        proj = dot(zn, w, True)
        gated = sigmoid(proj[:, width:]) * proj[:, :width]
        for i in range(n):
            at = slice(i * n, (i + 1) * n)
            pm = mj * mask_ref[i].astype(f32)
            dst[at, :] = (pm * gated[at]).astype(bf16).astype(f32)

    cot_relay(start, True)

    def products(step, start):
        sums = lax.fori_loop(0, n, step, ((start,) * rows,) * 2, unroll=24)
        return [jnp.concatenate(s, axis=0) for s in sums]

    def tri_step(k, sums):
        out = []
        for rows_ref, turned_ref, parts in ((l_s, r_s, sums[0]), (r_s, l_s, sums[1])):
            turned = turned_ref[pl.ds(k, n, stride=n), :]
            out.append(tuple(
                s + rows_ref[pl.ds((r * rows + i) * n + k, 1), :] * turned
                for i, s in enumerate(parts)
            ))
        return tuple(out)

    tri_a, tri_b = products(tri_step, jnp.zeros((n, width), f32))

    def turned_block(ref):
        return jnp.concatenate(
            [ref[pl.ds(r * rows + j, n, stride=n), :] for j in range(rows)], axis=0
        )

    def own_cells(ref, first):
        return jnp.concatenate(
            [ref[pl.ds((first + i) * n + c * cols, pad), :] for i in range(rows)], axis=0
        )

    def forward(tri, zn):
        mean, rstd = norm_stats(tri)
        xhat = (tri - mean) * rstd
        proj_out = dot(xhat.astype(bf16), w_out)
        gate = sigmoid(dot(zn, w_gate, True))
        return xhat, rstd, proj_out, gate

    def backward(xhat, rstd, gate, cot):
        dxn = dot((cot * gate).astype(bf16), w_out, True)
        dtri = (dxn - lane_mean(dxn) - xhat * lane_mean(dxn * xhat)) * rstd
        return dtri.astype(bf16).astype(f32)

    own_rows = pl.ds(pl.multiple_of(r * block, 8), block)
    xhat_a, rstd_a, proj_out, gate_a = forward(tri_a, zh_s[own_rows, :].astype(bf16))
    xhat_b, rstd_b, _, gate_b = forward(tri_b, turned_block(zh_s).astype(bf16))
    u_s[0:block, :] = gate_a * proj_out
    u_s[block:, :] = jnp.zeros((u_s.shape[0] - block, width), f32)
    dg_s[block:, :] = jnp.zeros((u_s.shape[0] - block, width), f32)

    z = own_cells(z_s, r * rows)
    mean, rstd = norm_stats(z)
    zhat = (z - mean) * rstd
    zn = zhat.astype(bf16)
    own_mask = mj_s[pl.ds(c * cols, pad), :]
    pm = jnp.concatenate(
        [own_mask * mask_ref[r * rows + i].astype(f32) for i in range(rows)], axis=0
    )
    factors = []
    for w in (w_left, w_right):
        proj = dot(zn, w, True)
        gated = pm * sigmoid(proj[:, width:])
        factors.append((gated, proj[:, :width] * gated * (1.0 - gated)))

    def put(i, value):
        value = jnp.where(h == 0, value, pltpu.roll(value, width // 2, 1))
        out_ref[i] = value.reshape(rows, pad, width)[:, 0:cols, 0 : width // 2].astype(bf16)

    put(0, own_cells(u_s, 0))

    far_copy(cbuf, (r, other_c), c_fwd.at[0], c_near.at[0], {"col": other_c}).wait_recv()

    @pl.when(c != wanted_c)
    def _():
        far_copy(obuf, (), c_fwd.at[1], c_near.at[1], {"col": other_c}).wait_recv()

    for bc in range(2):
        for piece in range(pieces):
            for part, full in enumerate(merge(cbuf[r, bc, 0, piece], cbuf[r, bc, 1, piece])):
                for t in range(half_rows):
                    first = (part * half_rows + t) * n + bc * cols + piece * rows
                    ca_s[first : first + rows, :] = full[t * rows : (t + 1) * rows]
    for br in range(n_row):
        theirs = [
            jnp.where(br == r, cbuf[r, wanted_c, bh, wanted_piece].astype(f32), obuf[br, bh].astype(f32))
            for bh in range(2)
        ]
        for part, full in enumerate(merge(*theirs)):
            first = (br * rows + part * half_rows) * rows
            cb_s[first : first + half_rows * rows, :] = full
    cot_a = ca_s[...]
    cot_b = jnp.concatenate([cb_s[pl.ds(j, n, stride=rows), :] for j in range(rows)], axis=0)
    dg_s[0:block, :] = cot_a * proj_out * gate_a * (1.0 - gate_a)
    da_s[...] = backward(xhat_a, rstd_a, gate_a, cot_a)
    db_s[...] = backward(xhat_b, rstd_b, gate_b, cot_b)

    def gradient_step(j, sums):
        out = []
        for d_ref, other_ref, parts in ((da_s, r_s, sums[0]), (db_s, l_s, sums[1])):
            other = other_ref[pl.ds(j * n + c * cols, pad), :]
            out.append(tuple(
                s + d_ref[pl.ds(i * n + j, 1), :] * other for i, s in enumerate(parts)
            ))
        return tuple(out)

    grads = products(gradient_step, jnp.zeros((pad, width), f32))
    dzn = dot(own_cells(dg_s, 0).astype(bf16), w_gate)
    for grad, (value, gate), w in zip(grads, factors, (w_left, w_right)):
        dzn = dzn + dot(jnp.concatenate([grad * value, grad * gate], axis=1).astype(bf16), w)
    put(1, (dzn - lane_mean(dzn) - zhat * lane_mean(dzn * zhat)) * rstd)
    for copy in sent:
        copy.wait_send()
    def finish(copy):
        copy.wait_send()

    cot_copies(finish)
    cot_relay(finish, False)


def gathered(n_row, pair, token_mask, w_in, w_gate, w_out, cotangent):
    f32, bf16 = jnp.float32, jnp.bfloat16
    rows, cols, chans = pair.shape
    n = rows * n_row
    width = 2 * chans
    vmem = pl.BlockSpec(memory_space=pltpu.VMEM)
    pair_shard, cot_shard = (rows // 2 * cols, width), (cols // rows, rows // 2 * rows, width)
    pair_shards = pltpu.VMEM((n_row, 2, 2) + pair_shard, bf16)
    cot_shards = pltpu.VMEM((n_row, 2, 2) + cot_shard, bf16)
    cells = pltpu.VMEM((n * n + 8, width), f32)
    block = pltpu.VMEM((rows * n, width), f32)
    block_and_tail = pltpu.VMEM((rows * n + 8, width), f32)
    dma = pltpu.SemaphoreType.DMA
    args = (pair, token_mask, w_in.transpose(1, 2, 0), w_gate.T, w_out, cotangent)
    args = [pltpu.with_memory_space_constraint(a, pltpu.HBM) for a in args]
    out = pl.pallas_call(
        functools.partial(kernel, n_row),
        out_shape=pltpu.VMEM((2,) + pair.shape, bf16),
        in_specs=[pl.BlockSpec(memory_space=pltpu.HBM)] * 6,
        out_specs=vmem,
        scratch_shapes=[
            pltpu.VMEM(pair.shape, bf16), pltpu.VMEM(pair.shape, bf16),
            pltpu.SMEM(token_mask.shape, jnp.int32), dma((7,)),
            pair_shards, cot_shards, pltpu.VMEM((n_row, 2) + cot_shard[1:], bf16), pltpu.VMEM((6, width, width), bf16),
            pltpu.VMEM(pair_shard, f32), pltpu.VMEM(cot_shard, f32),
            cells, cells, block, block, cells, cells, pltpu.VMEM((n + 8, width), f32),
            block_and_tail, block_and_tail, block, block,
            dma((n_row, 2)), dma((n_row, 2)), dma((n_row,)), dma((n_row,)),
            dma((n_row, 2)), dma((n_row, 2)), dma((2,)), dma((2,)),
            dma((2,)), dma((2,)),
        ],
        compiler_params=pltpu.CompilerParams(
            collective_id=0, has_side_effects=True, vmem_limit_bytes=24 * 2**20
        ),
    )(*args)
    return out[0], out[1]


def body(pair, token_mask, w_in, w_gate, w_out, cotangent):
    f32 = jnp.float32
    brain_float_half = jnp.bfloat16
    rows = pair.shape[0]
    cols = pair.shape[1]
    chans = pair.shape[2]
    width_c = w_in.shape[0]
    hidden_dev = w_in.shape[2]
    hidden_channel_width = hidden_dev * lax.axis_size("chan")
    row_start = lax.axis_index("row") * rows
    col_start = lax.axis_index("col") * cols
    chan_start = lax.axis_index("chan") * chans
    zfull = lax.all_gather(pair, "chan", axis=2, tiled=True).astype(f32)
    mean_z = jnp.sum(zfull, axis=-1, keepdims=True) / width_c
    square_z = jnp.sum(zfull * zfull, axis=-1, keepdims=True) / width_c
    rstd_z = lax.rsqrt(square_z - mean_z * mean_z + EPS)
    zhat = (zfull - mean_z) * rstd_z
    zn_b = zhat.astype(brain_float_half)
    proj = jnp.einsum("rkc,cqh->rkqh", zn_b, w_in, preferred_element_type=f32)
    maskf = token_mask.astype(f32)
    mask_rows = lax.dynamic_slice_in_dim(maskf, row_start, rows)
    mask_cols = lax.dynamic_slice_in_dim(maskf, col_start, cols)
    pmask = (mask_rows[:, None] * mask_cols[None, :])[..., None]
    sig_one = jax.nn.sigmoid(proj[:, :, 1])
    sig_three = jax.nn.sigmoid(proj[:, :, 3])
    left = (pmask * sig_one * proj[:, :, 0]).astype(brain_float_half)
    right = (pmask * sig_three * proj[:, :, 2]).astype(brain_float_half)
    partial_tri = jnp.einsum(
        "ikh,jkh->ijh",
        left,
        lax.all_gather(right, "row", axis=0, tiled=True),
        preferred_element_type=f32,
    )
    triangle_product = lax.psum_scatter(partial_tri, "col", scatter_dimension=1, tiled=True)
    sum_x, square_x = lax.psum(
        (jnp.sum(triangle_product, axis=-1), jnp.sum(triangle_product * triangle_product, axis=-1)),
        "chan",
    )
    input_mean = (sum_x / hidden_channel_width)[..., None]
    input_inverse_deviation = lax.rsqrt(
        square_x[..., None] / hidden_channel_width - input_mean * input_mean + EPS
    )
    centered_input = (triangle_product - input_mean) * input_inverse_deviation
    normed_input_low_precision = centered_input.astype(brain_float_half)
    out_term = jnp.einsum(
        "rch,hd->rcd", normed_input_low_precision, w_out, preferred_element_type=f32
    )
    proj_out = lax.psum_scatter(out_term, "chan", scatter_dimension=2, tiled=True)
    gate = jax.nn.sigmoid(jnp.einsum("rcd,de->rce", zn_b, w_gate, preferred_element_type=f32))
    update = (gate * proj_out).astype(brain_float_half)
    cot = cotangent.astype(f32)
    dproj = (cot * gate).astype(brain_float_half)
    dgate = (cot * proj_out * gate * (1.0 - gate)).astype(brain_float_half)
    dproj_all = lax.all_gather(dproj, "chan", axis=2, tiled=True)
    normed_input_gradient = jnp.einsum("rcd,hd->rch", dproj_all, w_out, preferred_element_type=f32)
    first_operand, second_operand = lax.psum(
        (
            jnp.sum(normed_input_gradient, axis=-1),
            jnp.sum(normed_input_gradient * centered_input, axis=-1),
        ),
        "chan",
    )
    triangle_gradient = (
        (
            normed_input_gradient
            - (first_operand / hidden_channel_width)[..., None]
            - centered_input * (second_operand / hidden_channel_width)[..., None]
        )
        * input_inverse_deviation
    ).astype(brain_float_half)
    dtri_rows = lax.all_gather(triangle_gradient, "col", axis=1, tiled=True)
    block = dtri_rows
    dleft = jnp.einsum(
        "ijh,jkh->ikh",
        block,
        lax.all_gather(right, "row", axis=0, tiled=True),
        preferred_element_type=f32,
    )
    dtri_turned = lax.all_to_all(dtri_rows, "row", split_axis=1, concat_axis=0, tiled=True)
    block = dtri_turned
    dright = jnp.einsum(
        "ijh,ikh->jkh",
        block,
        lax.all_gather(left, "row", axis=0, tiled=True),
        preferred_element_type=f32,
    )
    dpre = jnp.stack(
        [
            dleft * pmask * sig_one,
            dleft * pmask * proj[:, :, 0] * sig_one * (1.0 - sig_one),
            dright * pmask * sig_three,
            dright * pmask * proj[:, :, 2] * sig_three * (1.0 - sig_three),
        ],
        axis=2,
    ).astype(brain_float_half)
    dzn_term = jnp.einsum("rkqh,cqh->rkc", dpre, w_in, preferred_element_type=f32)
    dzn_term = dzn_term + jnp.einsum("rkd,cd->rkc", dgate, w_gate, preferred_element_type=f32)
    dzn = lax.psum_scatter(dzn_term, "chan", scatter_dimension=2, tiled=True)
    zhat_own = lax.dynamic_slice_in_dim(zhat, chan_start, chans, 2)
    first_z, second_z = lax.psum((jnp.sum(dzn, axis=-1), jnp.sum(dzn * zhat_own, axis=-1)), "chan")
    pair_grad = (
        (dzn - (first_z / width_c)[..., None] - zhat_own * (second_z / width_c)[..., None]) * rstd_z
    ).astype(brain_float_half)
    return (update, pair_grad)


def plan(pair, token_mask, w_in, w_gate, w_out, cotangent):
    n_row, n_col, n_chan = (lax.axis_size(a) for a in ("row", "col", "chan"))
    rows, cols, chans = pair.shape
    n = token_mask.shape[0]
    small = n <= 32 and n % 8 == 0 and rows % 2 == 0 and cols % 4 == 0 and rows * n % 16 == 0
    small = small and cols % rows == 0
    shaped = n_col == 2 and n_chan == 2 and chans == 64 and w_in.shape == (128, 4, 64)
    if small and shaped and -(-cols // 16) * 16 - cols <= 8:
        return gathered(n_row, pair, token_mask, w_in, w_gate, w_out, cotangent)
    return body(pair, token_mask, w_in, w_gate, w_out, cotangent)


def solution(mesh):
    return jax.shard_map(
        plan,
        mesh=mesh,
        in_specs=(
            P(("groups", "row"), "col", "chan"),
            P("groups"),
            P(None, None, "chan"),
            P(None, "chan"),
            P("chan", None),
            P(("groups", "row"), "col", "chan"),
        ),
        out_specs=(P(("groups", "row"), "col", "chan"), P(("groups", "row"), "col", "chan")),
        check_vma=False,
    )
```

```python
import functools

import jax
import jax.numpy as jnp
from jax import lax
from jax.experimental import pallas as pl
from jax.experimental.pallas import tpu as pltpu
from jax.sharding import PartitionSpec as P

EPS = 1e-05
MESH = pl.DeviceIdType.MESH


def sigmoid(x):
    return 1.0 / (1.0 + jnp.exp(-x))


def lane_mean(x):
    return jnp.sum(x, axis=-1, keepdims=True) * (1.0 / x.shape[-1])


def norm_stats(x):
    mean = lane_mean(x)
    return mean, lax.rsqrt(lane_mean(x * x) - mean * mean + EPS)


def merge(first, second):
    first, second = first.astype(jnp.float32), second.astype(jnp.float32)
    axis = first.ndim - 1
    width = first.shape[-1]
    low = lax.broadcasted_iota(jnp.int32, first.shape, axis) < width // 2
    return (
        jnp.where(low, first, pltpu.roll(second, width // 2, axis)),
        jnp.where(low, pltpu.roll(first, width // 2, axis), second),
    )


def dot(a, b, transposed=False):
    return lax.dot_general(
        a, b, (((1,), (1 if transposed else 0,)), ((), ())), preferred_element_type=jnp.float32
    )


def kernel(
    n_row, pair_hbm, mask_hbm, w_in_hbm, w_gate_hbm, w_out_hbm, cot_hbm, out_ref,
    pair_ref, cot_ref, mask_ref, in_sem, pbuf, cbuf, obuf, wbuf, pp_s, cp_s, z_s, zh_s, ca_s, cb_s, zd_s, pm_s, l_s, r_s, mj_s, u_s, dg_s, da_s, db_s,
    p_send, p_recv, p_fwd, p_near, c_send, c_recv, c_fwd, c_near, w_send, w_recv,
):
    f32, bf16 = jnp.float32, jnp.bfloat16
    rows, cols, _ = pair_ref.shape
    n = rows * n_row
    width = 2 * pair_ref.shape[2]
    half_rows = rows // 2
    pad = -(-cols // 16) * 16
    pieces = cols // rows
    block = rows * n
    r, c, h = lax.axis_index("row"), lax.axis_index("col"), lax.axis_index("chan")
    other_c, other_h = 1 - c, 1 - h
    wanted_c = lax.div(r * rows, cols)
    wanted_piece = r - wanted_c * (cols // rows)
    plane = [(0, 1), (1, 0), (1, 1)]

    def partner(dc, dh):
        return lax.rem(c + dc, 2), lax.rem(h + dh, 2)


    def place(dr, dh):
        return lax.rem(r + dr, n_row), lax.rem(h + dh, 2)

    steps = [(dr, dh) for dr in range(n_row) for dh in range(2)]
    far = [s for s in steps if s != (0, 0)]

    mine = pl.ds(pl.multiple_of(h * (width // 2), width // 2), width // 2)
    loads = [
        pltpu.make_async_copy(src, dst, in_sem.at[i])
        for i, (src, dst) in enumerate(
            [
                (pair_hbm, pair_ref),
                (w_in_hbm.at[0:2], wbuf.at[0:2, mine]),
                (w_gate_hbm, wbuf.at[2, mine]),
                (w_in_hbm.at[2:4], wbuf.at[3:5, mine]),
                (w_out_hbm, wbuf.at[5, mine]),
                (cot_hbm, cot_ref),
                (mask_hbm, mask_ref),
            ]
        )
    ]
    for load in loads:
        load.start()

    barrier = pltpu.get_barrier_semaphore()
    everyone = [(dr, 0, dh) for dr, dh in far] + [(0, 1, 0)]
    for dr, dc, dh in everyone:
        pc, ph = partner(dc, dh)
        device = {"row": lax.rem(r + dr, n_row), "col": pc, "chan": ph}
        pl.semaphore_signal(barrier, inc=1, device_id=device, device_id_type=MESH)

    def packed(ref):
        x = ref[...].astype(f32)
        return jnp.concatenate([x[:half_rows], x[half_rows:]], axis=-1)

    def pack_pair():
        x = packed(pair_ref)
        for t in range(half_rows):
            pp_s[t * cols : (t + 1) * cols, :] = x[t]
        pbuf[r, c, h] = pp_s[...].astype(bf16)

    def pack_cot():
        x = packed(cot_ref)
        for piece in range(pieces):
            for t in range(half_rows):
                cp_s[piece, t * rows : (t + 1) * rows, :] = x[t, piece * rows : (piece + 1) * rows]
            cbuf[r, c, h, piece] = cp_s[piece].astype(bf16)

    loads[0].wait()
    pack_pair()

    def far_copy(buf, slot, send, recv, device):
        part = buf.at[slot] if slot else buf
        return pltpu.make_async_remote_copy(
            src_ref=part, dst_ref=part, send_sem=send, recv_sem=recv,
            device_id=device, device_id_type=MESH,
        )

    def shard_copy(dr, dh):
        pr, ph = place(dr, dh)
        return far_copy(pbuf, (r, c, h), p_send.at[dr, dh], p_recv.at[r, h], {"row": pr, "chan": ph})

    def relay(dr):
        pr = lax.rem(r + dr, n_row)
        for dh in range(2):
            if (dr, dh) != (0, 0):
                ph = lax.rem(h + dh, 2)
                far_copy(pbuf, (pr, c, ph), p_send.at[dr, dh], p_recv.at[pr, ph], {"chan": ph}).wait_recv()
        return far_copy(pbuf, (pr, c), p_fwd.at[dr], p_near.at[dr], {"col": other_c})

    def cot_copies(act):
        act(far_copy(cbuf, (r, c, h), c_send.at[0, 1], c_recv.at[r, h], {"chan": other_h}))
        for dr in range(1, n_row):
            pr = lax.rem(r + dr, n_row)

            def to_row():
                for dh in range(2):
                    act(pltpu.make_async_remote_copy(
                        src_ref=cbuf.at[r, c, h, pr - c * pieces], dst_ref=obuf.at[r, h],
                        send_sem=c_send.at[dr, dh], recv_sem=c_recv.at[r, h],
                        device_id={"row": pr, "chan": lax.rem(h + dh, 2)}, device_id_type=MESH,
                    ))

            pl.when(lax.div(pr * rows, cols) == c)(to_row)

    def cot_relay(act, arrive):
        if arrive:
            far_copy(cbuf, (r, c, other_h), c_send.at[0, 1], c_recv.at[r, other_h], {"chan": other_h}).wait_recv()
        act(far_copy(cbuf, (r, c), c_fwd.at[0], c_near.at[0], {"col": other_c}))

        @pl.when(c == wanted_c)
        def _():
            if arrive:
                for dr in range(1, n_row):
                    pr = lax.rem(r + dr, n_row)
                    for ph in range(2):
                        far_copy(obuf, (pr, ph), c_send.at[0, 1], c_recv.at[pr, ph], {"chan": other_h}).wait_recv()
            act(far_copy(obuf, (), c_fwd.at[1], c_near.at[1], {"col": other_c}))

    def start(copy):
        copy.start()

    loads[5].wait()
    pack_cot()

    loads[6].wait()
    token = lax.broadcasted_iota(jnp.int32, (n, width), 0)
    mj = jnp.zeros((n, width), f32)
    for j in range(n):
        mj = jnp.where(token == j, mask_ref[j].astype(f32), mj)
    mj_s[...] = jnp.zeros(mj_s.shape, f32)
    mj_s[0:n, :] = mj
    for bc in range(2):
        for i in range(n):
            pm = mj[bc * cols : (bc + 1) * cols] * mask_ref[i].astype(f32)
            pm_s[bc, i * cols : (i + 1) * cols, :] = pm
    tail = z_s.shape[0] - n * n
    for s in (z_s, zh_s, l_s, r_s):
        s[n * n : n * n + tail, :] = jnp.zeros((tail, width), f32)
    obuf[r] = jnp.zeros(obuf.shape[1:], bf16)
    for load in loads[1:5]:
        load.wait()
    pl.semaphore_wait(barrier, len(everyone))
    direct = [shard_copy(dr, dh) for dr, dh in far]
    for copy in direct:
        copy.start()
    sent = []

    def weights(core, rows):
        return (pl.ds(3 * core, 3), rows)

    theirs = pl.ds(pl.multiple_of(other_h * (width // 2), width // 2), width // 2)
    w_far = far_copy(wbuf, weights(c, mine), w_send.at[0], w_recv.at[0], {"chan": other_h})
    w_far.start()
    cot_copies(start)
    sent.append(relay(0))
    sent[-1].start()
    w_near = far_copy(wbuf, weights(c, theirs), w_send.at[1], w_recv.at[1], {"col": other_c})
    far_copy(wbuf, weights(c, theirs), w_send.at[0], w_recv.at[0], {"chan": other_h}).wait_recv()
    w_near.start()
    sent.append(w_near)
    for dr in range(1, n_row):
        sent.append(relay(dr))
        sent[-1].start()
    for copy in direct + [w_far]:
        copy.wait_send()
    far_copy(wbuf, weights(other_c, theirs), w_send.at[1], w_recv.at[1], {"col": other_c}).wait_recv()

    w_left = wbuf[0:2].reshape(2 * width, width)
    w_right = wbuf[3:5].reshape(2 * width, width)
    w_gate, w_out = wbuf[2], wbuf[5]

    def unpack_pair(br, bc):
        for part, full in enumerate(merge(pbuf[br, bc, 0], pbuf[br, bc, 1])):
            for t in range(half_rows):
                first = pl.multiple_of(br * block, 8) + (part * half_rows + t) * n + bc * cols
                z_s[pl.ds(first, cols), :] = full[t * cols : (t + 1) * cols]

    def project(bc):
        for br in range(n_row):
            for part, full in enumerate(merge(pbuf[br, bc, 0], pbuf[br, bc, 1])):
                first = (br * rows + part * half_rows) * cols
                zd_s[first : first + half_rows * cols, :] = full
        z = zd_s[...]
        mean, rstd = norm_stats(z)
        zh = (z - mean) * rstd
        zn = zh.astype(bf16)
        pm = pm_s[bc]
        results = [(z_s, z), (zh_s, zh)]
        for w, dst in ((w_left, l_s), (w_right, r_s)):
            proj = dot(zn, w, True)
            value = pm * sigmoid(proj[:, width:]) * proj[:, :width]
            results.append((dst, value.astype(bf16).astype(f32)))
        for dst, value in results:
            zd_s[...] = value
            for i in range(n):
                dst[pl.ds(i * n + bc * cols, cols), :] = zd_s[i * cols : (i + 1) * cols, :]

    project(c)
    for dr in range(n_row):
        slot = (lax.rem(r + dr, n_row), other_c)
        far_copy(pbuf, slot, p_fwd.at[dr], p_near.at[dr], {"col": other_c}).wait_recv()
    cot_relay(start, True)
    project(other_c)


    def products(step, start):
        sums = lax.fori_loop(0, n, step, ((start,) * rows,) * 2, unroll=24)
        return [jnp.concatenate(s, axis=0) for s in sums]

    def tri_step(k, sums):
        out = []
        for rows_ref, turned_ref, parts in ((l_s, r_s, sums[0]), (r_s, l_s, sums[1])):
            turned = turned_ref[pl.ds(k, n, stride=n), :]
            out.append(tuple(
                s + rows_ref[pl.ds((r * rows + i) * n + k, 1), :] * turned
                for i, s in enumerate(parts)
            ))
        return tuple(out)

    tri_a, tri_b = products(tri_step, jnp.zeros((n, width), f32))

    def turned_block(ref):
        return jnp.concatenate(
            [ref[pl.ds(r * rows + j, n, stride=n), :] for j in range(rows)], axis=0
        )

    def own_cells(ref, first):
        return jnp.concatenate(
            [ref[pl.ds((first + i) * n + c * cols, pad), :] for i in range(rows)], axis=0
        )

    def forward(tri, zn):
        mean, rstd = norm_stats(tri)
        xhat = (tri - mean) * rstd
        proj_out = dot(xhat.astype(bf16), w_out)
        gate = sigmoid(dot(zn, w_gate, True))
        return xhat, rstd, proj_out, gate

    def backward(xhat, rstd, gate, cot):
        dxn = dot((cot * gate).astype(bf16), w_out, True)
        dtri = (dxn - lane_mean(dxn) - xhat * lane_mean(dxn * xhat)) * rstd
        return dtri.astype(bf16).astype(f32)

    own_rows = pl.ds(pl.multiple_of(r * block, 8), block)
    xhat_a, rstd_a, proj_out, gate_a = forward(tri_a, zh_s[own_rows, :].astype(bf16))
    xhat_b, rstd_b, _, gate_b = forward(tri_b, turned_block(zh_s).astype(bf16))
    u_s[0:block, :] = gate_a * proj_out
    u_s[block:, :] = jnp.zeros((u_s.shape[0] - block, width), f32)
    dg_s[block:, :] = jnp.zeros((u_s.shape[0] - block, width), f32)

    z = own_cells(z_s, r * rows)
    mean, rstd = norm_stats(z)
    zhat = (z - mean) * rstd
    zn = zhat.astype(bf16)
    own_mask = mj_s[pl.ds(c * cols, pad), :]
    pm = jnp.concatenate(
        [own_mask * mask_ref[r * rows + i].astype(f32) for i in range(rows)], axis=0
    )
    factors = []
    for w in (w_left, w_right):
        proj = dot(zn, w, True)
        gated = pm * sigmoid(proj[:, width:])
        factors.append((gated, proj[:, :width] * gated * (1.0 - gated)))

    def put(i, value):
        value = jnp.where(h == 0, value, pltpu.roll(value, width // 2, 1))
        out_ref[i] = value.reshape(rows, pad, width)[:, 0:cols, 0 : width // 2].astype(bf16)

    put(0, own_cells(u_s, 0))

    far_copy(cbuf, (r, other_c), c_fwd.at[0], c_near.at[0], {"col": other_c}).wait_recv()

    @pl.when(c != wanted_c)
    def _():
        far_copy(obuf, (), c_fwd.at[1], c_near.at[1], {"col": other_c}).wait_recv()

    for bc in range(2):
        for piece in range(pieces):
            for part, full in enumerate(merge(cbuf[r, bc, 0, piece], cbuf[r, bc, 1, piece])):
                for t in range(half_rows):
                    first = (part * half_rows + t) * n + bc * cols + piece * rows
                    ca_s[first : first + rows, :] = full[t * rows : (t + 1) * rows]
    for br in range(n_row):
        theirs = [
            jnp.where(br == r, cbuf[r, wanted_c, bh, wanted_piece].astype(f32), obuf[br, bh].astype(f32))
            for bh in range(2)
        ]
        for part, full in enumerate(merge(*theirs)):
            first = (br * rows + part * half_rows) * rows
            cb_s[first : first + half_rows * rows, :] = full
    cot_a = ca_s[...]
    cot_b = jnp.concatenate([cb_s[pl.ds(j, n, stride=rows), :] for j in range(rows)], axis=0)
    dg_s[0:block, :] = cot_a * proj_out * gate_a * (1.0 - gate_a)
    da_s[...] = backward(xhat_a, rstd_a, gate_a, cot_a)
    db_s[...] = backward(xhat_b, rstd_b, gate_b, cot_b)

    def gradient_step(j, sums):
        out = []
        for d_ref, other_ref, parts in ((da_s, r_s, sums[0]), (db_s, l_s, sums[1])):
            other = other_ref[pl.ds(j * n + c * cols, pad), :]
            out.append(tuple(
                s + d_ref[pl.ds(i * n + j, 1), :] * other for i, s in enumerate(parts)
            ))
        return tuple(out)

    grads = products(gradient_step, jnp.zeros((pad, width), f32))
    dzn = dot(own_cells(dg_s, 0).astype(bf16), w_gate)
    for grad, (value, gate), w in zip(grads, factors, (w_left, w_right)):
        dzn = dzn + dot(jnp.concatenate([grad * value, grad * gate], axis=1).astype(bf16), w)
    put(1, (dzn - lane_mean(dzn) - zhat * lane_mean(dzn * zhat)) * rstd)
    for copy in sent:
        copy.wait_send()
    def finish(copy):
        copy.wait_send()

    cot_copies(finish)
    cot_relay(finish, False)


def gathered(n_row, pair, token_mask, w_in, w_gate, w_out, cotangent):
    f32, bf16 = jnp.float32, jnp.bfloat16
    rows, cols, chans = pair.shape
    n = rows * n_row
    width = 2 * chans
    vmem = pl.BlockSpec(memory_space=pltpu.VMEM)
    pair_shard, cot_shard = (rows // 2 * cols, width), (cols // rows, rows // 2 * rows, width)
    pair_shards = pltpu.VMEM((n_row, 2, 2) + pair_shard, bf16)
    cot_shards = pltpu.VMEM((n_row, 2, 2) + cot_shard, bf16)
    cells = pltpu.VMEM((n * n + 8, width), f32)
    block = pltpu.VMEM((rows * n, width), f32)
    block_and_tail = pltpu.VMEM((rows * n + 8, width), f32)
    dma = pltpu.SemaphoreType.DMA
    args = (pair, token_mask, w_in.transpose(1, 2, 0), w_gate.T, w_out, cotangent)
    args = [pltpu.with_memory_space_constraint(a, pltpu.HBM) for a in args]
    out = pl.pallas_call(
        functools.partial(kernel, n_row),
        out_shape=pltpu.VMEM((2,) + pair.shape, bf16),
        in_specs=[pl.BlockSpec(memory_space=pltpu.HBM)] * 6,
        out_specs=vmem,
        scratch_shapes=[
            pltpu.VMEM(pair.shape, bf16), pltpu.VMEM(pair.shape, bf16),
            pltpu.SMEM(token_mask.shape, jnp.int32), dma((7,)),
            pair_shards, cot_shards, pltpu.VMEM((n_row, 2) + cot_shard[1:], bf16), pltpu.VMEM((6, width, width), bf16),
            pltpu.VMEM(pair_shard, f32), pltpu.VMEM(cot_shard, f32),
            cells, cells, block, block, pltpu.VMEM((n * cols, width), f32), pltpu.VMEM((2, n * cols, width), f32), cells, cells, pltpu.VMEM((n + 8, width), f32),
            block_and_tail, block_and_tail, block, block,
            dma((n_row, 2)), dma((n_row, 2)), dma((n_row,)), dma((n_row,)),
            dma((n_row, 2)), dma((n_row, 2)), dma((2,)), dma((2,)),
            dma((2,)), dma((2,)),
        ],
        compiler_params=pltpu.CompilerParams(
            collective_id=0, has_side_effects=True, vmem_limit_bytes=24 * 2**20
        ),
    )(*args)
    return out[0], out[1]


def body(pair, token_mask, w_in, w_gate, w_out, cotangent):
    f32 = jnp.float32
    brain_float_half = jnp.bfloat16
    rows = pair.shape[0]
    cols = pair.shape[1]
    chans = pair.shape[2]
    width_c = w_in.shape[0]
    hidden_dev = w_in.shape[2]
    hidden_channel_width = hidden_dev * lax.axis_size("chan")
    row_start = lax.axis_index("row") * rows
    col_start = lax.axis_index("col") * cols
    chan_start = lax.axis_index("chan") * chans
    zfull = lax.all_gather(pair, "chan", axis=2, tiled=True).astype(f32)
    mean_z = jnp.sum(zfull, axis=-1, keepdims=True) / width_c
    square_z = jnp.sum(zfull * zfull, axis=-1, keepdims=True) / width_c
    rstd_z = lax.rsqrt(square_z - mean_z * mean_z + EPS)
    zhat = (zfull - mean_z) * rstd_z
    zn_b = zhat.astype(brain_float_half)
    proj = jnp.einsum("rkc,cqh->rkqh", zn_b, w_in, preferred_element_type=f32)
    maskf = token_mask.astype(f32)
    mask_rows = lax.dynamic_slice_in_dim(maskf, row_start, rows)
    mask_cols = lax.dynamic_slice_in_dim(maskf, col_start, cols)
    pmask = (mask_rows[:, None] * mask_cols[None, :])[..., None]
    sig_one = jax.nn.sigmoid(proj[:, :, 1])
    sig_three = jax.nn.sigmoid(proj[:, :, 3])
    left = (pmask * sig_one * proj[:, :, 0]).astype(brain_float_half)
    right = (pmask * sig_three * proj[:, :, 2]).astype(brain_float_half)
    partial_tri = jnp.einsum(
        "ikh,jkh->ijh",
        left,
        lax.all_gather(right, "row", axis=0, tiled=True),
        preferred_element_type=f32,
    )
    triangle_product = lax.psum_scatter(partial_tri, "col", scatter_dimension=1, tiled=True)
    sum_x, square_x = lax.psum(
        (jnp.sum(triangle_product, axis=-1), jnp.sum(triangle_product * triangle_product, axis=-1)),
        "chan",
    )
    input_mean = (sum_x / hidden_channel_width)[..., None]
    input_inverse_deviation = lax.rsqrt(
        square_x[..., None] / hidden_channel_width - input_mean * input_mean + EPS
    )
    centered_input = (triangle_product - input_mean) * input_inverse_deviation
    normed_input_low_precision = centered_input.astype(brain_float_half)
    out_term = jnp.einsum(
        "rch,hd->rcd", normed_input_low_precision, w_out, preferred_element_type=f32
    )
    proj_out = lax.psum_scatter(out_term, "chan", scatter_dimension=2, tiled=True)
    gate = jax.nn.sigmoid(jnp.einsum("rcd,de->rce", zn_b, w_gate, preferred_element_type=f32))
    update = (gate * proj_out).astype(brain_float_half)
    cot = cotangent.astype(f32)
    dproj = (cot * gate).astype(brain_float_half)
    dgate = (cot * proj_out * gate * (1.0 - gate)).astype(brain_float_half)
    dproj_all = lax.all_gather(dproj, "chan", axis=2, tiled=True)
    normed_input_gradient = jnp.einsum("rcd,hd->rch", dproj_all, w_out, preferred_element_type=f32)
    first_operand, second_operand = lax.psum(
        (
            jnp.sum(normed_input_gradient, axis=-1),
            jnp.sum(normed_input_gradient * centered_input, axis=-1),
        ),
        "chan",
    )
    triangle_gradient = (
        (
            normed_input_gradient
            - (first_operand / hidden_channel_width)[..., None]
            - centered_input * (second_operand / hidden_channel_width)[..., None]
        )
        * input_inverse_deviation
    ).astype(brain_float_half)
    dtri_rows = lax.all_gather(triangle_gradient, "col", axis=1, tiled=True)
    block = dtri_rows
    dleft = jnp.einsum(
        "ijh,jkh->ikh",
        block,
        lax.all_gather(right, "row", axis=0, tiled=True),
        preferred_element_type=f32,
    )
    dtri_turned = lax.all_to_all(dtri_rows, "row", split_axis=1, concat_axis=0, tiled=True)
    block = dtri_turned
    dright = jnp.einsum(
        "ijh,ikh->jkh",
        block,
        lax.all_gather(left, "row", axis=0, tiled=True),
        preferred_element_type=f32,
    )
    dpre = jnp.stack(
        [
            dleft * pmask * sig_one,
            dleft * pmask * proj[:, :, 0] * sig_one * (1.0 - sig_one),
            dright * pmask * sig_three,
            dright * pmask * proj[:, :, 2] * sig_three * (1.0 - sig_three),
        ],
        axis=2,
    ).astype(brain_float_half)
    dzn_term = jnp.einsum("rkqh,cqh->rkc", dpre, w_in, preferred_element_type=f32)
    dzn_term = dzn_term + jnp.einsum("rkd,cd->rkc", dgate, w_gate, preferred_element_type=f32)
    dzn = lax.psum_scatter(dzn_term, "chan", scatter_dimension=2, tiled=True)
    zhat_own = lax.dynamic_slice_in_dim(zhat, chan_start, chans, 2)
    first_z, second_z = lax.psum((jnp.sum(dzn, axis=-1), jnp.sum(dzn * zhat_own, axis=-1)), "chan")
    pair_grad = (
        (dzn - (first_z / width_c)[..., None] - zhat_own * (second_z / width_c)[..., None]) * rstd_z
    ).astype(brain_float_half)
    return (update, pair_grad)


def plan(pair, token_mask, w_in, w_gate, w_out, cotangent):
    n_row, n_col, n_chan = (lax.axis_size(a) for a in ("row", "col", "chan"))
    rows, cols, chans = pair.shape
    n = token_mask.shape[0]
    small = n <= 32 and n % 8 == 0 and rows % 2 == 0 and cols % 4 == 0 and rows * n % 16 == 0
    small = small and cols % rows == 0
    shaped = n_col == 2 and n_chan == 2 and chans == 64 and w_in.shape == (128, 4, 64)
    if small and shaped and -(-cols // 16) * 16 - cols <= 8:
        return gathered(n_row, pair, token_mask, w_in, w_gate, w_out, cotangent)
    return body(pair, token_mask, w_in, w_gate, w_out, cotangent)


def solution(mesh):
    return jax.shard_map(
        plan,
        mesh=mesh,
        in_specs=(
            P(("groups", "row"), "col", "chan"),
            P("groups"),
            P(None, None, "chan"),
            P(None, "chan"),
            P("chan", None),
            P(("groups", "row"), "col", "chan"),
        ),
        out_specs=(P(("groups", "row"), "col", "chan"), P(("groups", "row"), "col", "chan")),
        check_vma=False,
    )
```
